256 devices in a mesh: img: 8 (over y, core), txt: 32 (over x, z).
Axes of the slice: x: 4, y: 4, z: 8, core: 2. Of those that a mesh axis runs over, the one named last changes fastest.
Arguments:
- picture_embeddings: bfloat16 [16384, 1152], P(('img', 'txt')), may hold values from -4 to 4
- caption_embeddings: bfloat16 [16384, 1152], P(('txt', 'img')), may hold values from -4 to 4
- sharpness_factor: float32 [1], replicated, may hold values from 24 to 32
- pairing_shift: float32 [1], replicated, may hold values from -7 to -5
Outputs:
- loss: float32 [1], replicated
- image_grad: float32 [16384, 1152], P(('img', 'txt'))
- text_grad: float32 [16384, 1152], P(('txt', 'img'))
The draws below stay inside these ranges and needn't reach their ends.
All inputs are finite; a program needn't handle non-finite values.
Results may differ from the reference program's by a relative error of at most 0.0016.
Values may be sent and summed in bfloat16 or wider, within the bound.
A program may use at most 64 MiB of HBM per device.

```python
import math
import jax
import jax.numpy as jnp
from jax import lax

D = 1152
BATCH = 16384


def shared_parts(key):
    pair_key = jax.random.fold_in(key, 101)
    common_key = jax.random.fold_in(key, 102)
    strength_key = jax.random.fold_in(key, 103)
    dispersion_seed = jax.random.fold_in(key, 104)
    strength = jax.random.uniform(strength_key, (BATCH, 1), jnp.float32, 0.35, 0.7)
    paired = jax.random.truncated_normal(pair_key, -4.0, 4.0, (BATCH, D), jnp.float32) * D ** (-0.5) * strength
    common = jax.random.truncated_normal(common_key, -4.0, 4.0, (1, D), jnp.float32) * D ** (-0.5)
    spread_logs = jax.random.uniform(dispersion_seed, (1, D), jnp.float32, 0.0, math.log(8.0))
    spread = jnp.exp(spread_logs) * 0.257
    return (paired, common, spread)


def build_rows(key, noise, paired, common, spread, lowest, highest, shared_multiplier):
    logit_scale_key = jax.random.fold_in(key, 8)
    logs = jax.random.uniform(logit_scale_key, (BATCH, 1), jnp.float32, math.log(lowest), math.log(highest))
    rows = (paired + shared_multiplier * common + noise) * spread * jnp.exp(logs)
    return jnp.clip(rows, -4.0, 4.0)


def draw_picture_embeddings(key, part):
    paired, common, spread = shared_parts(key)
    key = jax.random.fold_in(key, 1)
    noise_key = jax.random.fold_in(key, 7)
    noise = jax.random.truncated_normal(noise_key, -4.0, 4.0, (BATCH, D), jnp.float32) * D ** (-0.5)
    return build_rows(key, noise, paired, common, spread, 4.0, 12.0, 0.25).astype(jnp.bfloat16)


def draw_caption_embeddings(key, part):
    paired, common, spread = shared_parts(key)
    key = jax.random.fold_in(key, 2)
    noise_key = jax.random.fold_in(key, 7)
    noise = jax.random.truncated_normal(noise_key, -4.0, 4.0, (BATCH, D), jnp.float32) * D ** (-0.5)
    return build_rows(key, noise, paired, common, spread, 4.0, 12.0, 0.25).astype(jnp.bfloat16)


def setup_inputs(seed: int = 0) -> dict:
    splits = jax.random.split(jax.random.key(seed), 5)
    picture_embeddings = draw_picture_embeddings(jax.random.fold_in(splits[4], 71), 0)
    caption_embeddings = draw_caption_embeddings(jax.random.fold_in(splits[4], 71), 0)
    sharpness_factor = jnp.clip(jax.random.uniform(splits[2], (1,), jnp.float32, 24.0, 32.0), 24.0, 32.0)
    pairing_shift = jnp.clip(jax.random.uniform(splits[3], (1,), jnp.float32, -7.0, -5.0), -7.0, -5.0)
    return dict(picture_embeddings=picture_embeddings, caption_embeddings=caption_embeddings, sharpness_factor=sharpness_factor, pairing_shift=pairing_shift)


def unit_normalize(raw):
    values = raw.astype(jnp.float32)
    inverse = lax.rsqrt(lax.optimization_barrier(jnp.sum(values * values, axis=1, keepdims=True)) + 1e-06)
    return (values, inverse, (values * inverse).astype(jnp.bfloat16))

def restore(values, inverse, grads):
    inner = lax.optimization_barrier(jnp.sum(values * grads, axis=1, keepdims=True))
    return inverse * grads - inverse * inverse * inverse * values * inner

def reference(picture_embeddings, caption_embeddings, sharpness_factor, pairing_shift):
    x_vals, x_inv, xn = unit_normalize(picture_embeddings)
    y_vals, y_inv, yn = unit_normalize(caption_embeddings)
    inverse_warmth_factor = sharpness_factor[0]
    shift = pairing_shift[0]
    block = math.gcd(BATCH, 512)
    steps = BATCH // block
    columns = jnp.arange(BATCH, dtype=jnp.int32)[None, :]

    def single_block_loss(carry, index):
        total, text_acc = carry
        start = (index * block).astype(jnp.int32)
        image_row_block = lax.dynamic_slice_in_dim(xn, start, block, 0)
        dots = jnp.dot(image_row_block, yn.T, preferred_element_type=jnp.float32)
        logits = inverse_warmth_factor * dots + shift
        rows = start + jnp.arange(block, dtype=jnp.int32)[:, None]
        positive = rows == columns
        label = jnp.where(positive, 1.0, -1.0).astype(jnp.float32)
        terms = jax.nn.softplus(-label * logits)
        weight = (jax.nn.sigmoid(logits) - positive.astype(jnp.float32)).astype(jnp.bfloat16)
        grad_rows = inverse_warmth_factor * jnp.dot(weight, yn, preferred_element_type=jnp.float32)
        text_part = lax.dot_general(weight, image_row_block, (((0,), (0,)), ((), ())), preferred_element_type=jnp.float32)
        return ((total + jnp.sum(terms), text_acc + inverse_warmth_factor * text_part), grad_rows)
    init = (jnp.zeros((), jnp.float32), jnp.zeros((BATCH, D), jnp.float32))
    (total, gyn), gx_blocks = lax.scan(single_block_loss, init, jnp.arange(steps, dtype=jnp.int32))
    gxn = gx_blocks.reshape(BATCH, D)
    loss = (total / BATCH).reshape(1)
    return (loss, restore(x_vals, x_inv, gxn), restore(y_vals, y_inv, gyn))
```

```python
import jax
import jax.numpy as jnp
from jax import lax
from jax.experimental import pallas as pl
from jax.experimental.pallas import tpu as pltpu
from jax.sharding import PartitionSpec as P

MESH = pl.DeviceIdType.MESH
F32 = jnp.float32
BF16 = jnp.bfloat16
ROWS = 64
HALF = 32
D = 1152
POS = {0: 0, 4: 1, 1: 2, 7: 3, 2: 4, 6: 5, 3: 6, 5: 7}


def encode(v):
    return (v * jnp.abs(v)).astype(BF16)


def decode(u):
    u = u.astype(F32)
    return u * lax.rsqrt(jnp.maximum(jnp.abs(u), 1e-37))


def kernel(x_ref, y_ref, scale_ref, shift_ref, loss_ref, gx_ref, gy_ref,
           xg, yg, w, own, isend, irecv, p2, p2send, p2recv, tf, crecv, zsend, zrecv,
           lacc, lsum, lrecv, ssem, rsem):
    img, txt = lax.axis_index("img"), lax.axis_index("txt")
    Y, C = img // 2, img % 2
    X, Z = txt // 8, txt % 8

    def dev(dx=0, dy=0, dz=0, dc=0):
        return (((Y + dy) % 4) * 2 + (C + dc) % 2, ((X + dx) % 4) * 8 + (Z + dz) % 8)

    count = [0]

    def copy(src, dst, to):
        i = count[0]
        count[0] += 1
        c = pltpu.make_async_remote_copy(src_ref=src, dst_ref=dst, send_sem=ssem.at[i], recv_sem=rsem.at[i],
                                         device_id=to, device_id_type=MESH)
        started.append(c)
        return c

    started = []
    barrier = pltpu.get_barrier_semaphore()
    peers = ([dev(dx=i) for i in (1, 2, 3)] + [dev(dy=i) for i in (1, 2, 3)]
             + [dev(dz=i) for i in range(1, 8)] + [dev(dc=1)])
    for p in peers:
        pl.semaphore_signal(barrier, inc=1, device_id=p, device_id_type=MESH)

    def unit(ref):
        values = ref[...].astype(F32)
        inverse = lax.rsqrt(jnp.sum(values * values, axis=1, keepdims=True) + 1e-06)
        return (values * inverse).astype(BF16)

    def A(k, j):
        return k * 256 + j * HALF

    def B(k, j):
        return k * 256 + 128 + j * HALF

    def yrow(s, rc):
        return POS[s] * 128 + rc * ROWS

    yn = unit(y_ref)
    yg[pl.ds(yrow(0, 0), ROWS)] = yn
    xn = unit(x_ref)
    xg[pl.ds(A(0, 0), HALF)] = xn[:HALF]
    xg[pl.ds(B(0, 0), HALF)] = xn[HALF:]
    pl.semaphore_wait(barrier, len(peers))

    def ydma(s_from, s_to, h, dz):
        return copy(yg.at[pl.ds(yrow(s_from, 0) + h * HALF, HALF)], yg.at[pl.ds(yrow(s_to, 0) + h * HALF, HALF)], dev(dz=dz))

    def xdma(a, b, n, to):
        return copy(xg.at[pl.ds(a, n)], xg.at[pl.ds(b, n)], to)

    def ycore(s):
        c = copy(yg.at[pl.ds(yrow(s, 0), ROWS)], yg.at[pl.ds(yrow(s, 1), ROWS)], dev(dc=1))
        c.start()
        return c

    up, down, cores = {}, {}, {}
    for h in (0, 1):
        up[1, h] = ydma(0, 7, h, 1)
        down[1, h] = ydma(0, 1, h, -1)
        up[1, h].start()
        down[1, h].start()
    fa, fb = {}, {}
    for j, d in ((3, 1), (1, -1), (2, 2)):
        fa[j] = xdma(A(0, 0), A(0, j), HALF, dev(dx=d))
        fb[j] = xdma(B(0, 0), B(0, j), HALF, dev(dy=d))
        fa[j].start()
        fb[j].start()
    sa, sb = {}, {}

    def second(j):
        for k, d in ((3, 1), (1, -1)):
            sa[k, j] = xdma(A(0, j), A(k, j), HALF, dev(dy=d))
            sb[k, j] = xdma(B(0, j), B(k, j), HALF, dev(dx=d))
            sa[k, j].start()
            sb[k, j].start()

    ta, tb = {}, {}

    def third(j):
        for k, d, o in ((3, 1, 16), (1, -1, 0)):
            sa[k, j].wait_recv()
            ta[k, j] = xdma(A(k, j) + o, A(2, j) + o, 16, dev(dy=d))
            ta[k, j].start()
            sb[k, j].wait_recv()
            tb[k, j] = xdma(B(k, j) + o, B(2, j) + o, 16, dev(dx=d))
            tb[k, j].start()

    def ystep(t):
        for h in (0, 1):
            if t <= 4:
                up[t - 1, h].wait_recv()
                if t < 4 or h == 0:
                    up[t, h] = ydma((9 - t) % 8, 8 - t, h, 1)
                    up[t, h].start()
                down[t - 1, h].wait_recv()
                if t < 4 or h == 1:
                    down[t, h] = ydma(t - 1, t, h, -1)
                    down[t, h].start()
        if t == 5:
            up[4, 0].wait_recv()
            down[4, 1].wait_recv()
            cores[4] = ycore(4)
        else:
            cores[9 - t] = ycore(9 - t)
            cores[t - 1] = ycore(t - 1)

    second(0)
    cores[0] = ycore(0)
    for j in (1, 3):
        fa[j].wait_recv()
        fb[j].wait_recv()
        second(j)
    ystep(2)
    fa[2].wait_recv()
    fb[2].wait_recv()
    second(2)
    third(0)
    ystep(3)
    third(1)
    ystep(4)
    third(3)
    ystep(5)
    third(2)
    for j in range(4):
        for k in (1, 3):
            ta[k, j].wait_recv()
            tb[k, j].wait_recv()
    for s in range(8):
        cores[s].wait_recv()

    scale = scale_ref[0]
    shift = shift_ref[0]
    lacc[...] = jnp.zeros_like(lacc)

    def tile(i, _):
        k = pl.multiple_of((i // 4) * 256, 256)
        g = pl.multiple_of((i % 4) * 256, 256)
        dots = lax.dot_general(xg[pl.ds(k, 256), :], yg[pl.ds(g, 256), :], (((1,), (1,)), ((), ())),
                               preferred_element_type=F32)
        e = jnp.exp(scale * dots + shift)
        d = 1.0 + e
        w[pl.ds(k, 256), pl.ds(g, 256)] = (e / d).astype(BF16)
        lacc[...] += jnp.sum(jnp.log1p(e).reshape(32, 8, 256), axis=0)
        return 0

    lax.fori_loop(0, 16, tile, 0)

    @pl.when(Y == Z // 2)
    def _():
        rc = (Z + C) % 2
        for xx in range(4):
            for h in (0, 1):
                k, j = (X - Y + 4) % 4, (xx - X + 4) % 4
                row = k * 256 + j * HALF if h == 0 else j * 256 + 128 + k * HALF
                row = pl.multiple_of(row, HALF)
                s = (4 * C + xx - Z + 8) % 8
                pos = jnp.where(s == 0, 0, jnp.where(s == 4, 1, jnp.where(s < 4, 2 * s, 2 * (8 - s) + 1)))
                col = pl.multiple_of(pos * 128, 128)
                yr = pl.multiple_of(pos * 128 + rc * ROWS + h * HALF, HALF)
                xv = xg[pl.ds(row, HALF), :].astype(F32)
                yv = yg[pl.ds(yr, HALF), :].astype(F32)
                z = scale * jnp.sum(xv * yv, axis=1, keepdims=True) + shift
                e = jnp.exp(z)
                wd = (e / (1.0 + e) - 1.0).astype(BF16)
                lane = lax.broadcasted_iota(jnp.int32, (HALF, 128), 1)
                sub = lax.broadcasted_iota(jnp.int32, (HALF, 128), 0)
                hit = lane == sub + rc * ROWS + h * HALF
                old = w[pl.ds(row, HALF), pl.ds(col, 128)]
                w[pl.ds(row, HALF), pl.ds(col, 128)] = jnp.where(hit, wd.astype(F32), old.astype(F32)).astype(BF16)
                zz = jnp.where(hit, z, 0.0)
                lacc[:, :128] -= jnp.sum(zz.reshape(4, 8, 128), axis=0)

    lcopies = {}

    def lsend(axis):
        n, me, base, kw = {"c": (2, C, 0, "dc"), "z": (8, Z, 2, "dz"), "x": (4, X, 10, "dx"), "y": (4, Y, 14, "dy")}[axis]
        v = jnp.sum(lacc[...]) if axis == "c" else lsum[0, 0]
        lrecv[base + me] = jnp.full((8, 128), v, F32)
        for o in range(1, n):
            c = copy(lrecv.at[base + me], lrecv.at[base + me], dev(**{kw: o}))
            c.start()
            lcopies[axis, o] = c

    def lwait(axis):
        n, base = {"c": (2, 0), "z": (8, 2), "x": (4, 10), "y": (4, 14)}[axis]
        for o in range(1, n):
            lcopies[axis, o].wait_recv()
        t = lrecv[base]
        for o in range(1, n):
            t = t + lrecv[base + o]
        lsum[...] = t

    lsend("c")

    cr = {}

    def text(g):
        tf[pl.ds(g * 256, 256), :] = lax.dot_general(w[:, pl.ds(g * 256, 256)], xg[...], (((0,), (0,)), ((), ())),
                                                     preferred_element_type=F32)
        for s in range(8):
            if POS[s] // 2 == g:
                cr[s] = copy(tf.at[pl.ds(yrow(s, 1), ROWS)], crecv.at[pl.ds(s * ROWS, ROWS)], dev(dc=1))
                cr[s].start()

    pa, pb = {}, {}

    def image(k):
        part = jnp.dot(w[pl.ds(k * 256, 256), :], yg[...], preferred_element_type=F32)
        if k == 0:
            own[...] = part
            return
        o = (k - 1) * 256
        isend[pl.ds(o, 256), :] = encode(part)
        pa[k] = copy(isend.at[pl.ds(o, 128)], irecv.at[pl.ds(o, 128)], dev(dy=k))
        pb[k] = copy(isend.at[pl.ds(o + 128, 128)], irecv.at[pl.ds(o + 128, 128)], dev(dx=k))
        pa[k].start()
        pb[k].start()

    def add_core(s):
        cr[s].wait_recv()
        tf[pl.ds(yrow(s, 0), ROWS), :] += crecv[pl.ds(s * ROWS, ROWS), :]

    zc = {}
    zslots = {}

    def zhop(direction, t, h):
        s = t if direction > 0 else 8 - t
        v = tf[pl.ds(yrow(s, 0) + h * HALF, HALF), :]
        first = 4 if (direction > 0) == (h == 0) else 3
        if t < first:
            zc[direction, t + 1, h].wait_recv()
            r = zslots[direction, t + 1, h]
            v = v + decode(zrecv[pl.ds(r, HALF), :])
        r = len(zslots) * HALF
        zslots[direction, t, h] = r
        zsend[pl.ds(r, HALF), :] = encode(v)
        zc[direction, t, h] = copy(zsend.at[pl.ds(r, HALF)], zrecv.at[pl.ds(r, HALF)], dev(dz=direction))
        zc[direction, t, h].start()

    text(0)
    image(2)
    add_core(4)
    add_core(0)
    zhop(1, 4, 0)
    zhop(-1, 4, 1)
    text(3)
    lwait("c")
    lsend("z")
    add_core(3)
    add_core(5)
    zhop(1, 3, 1)
    zhop(-1, 3, 0)
    image(1)
    image(3)
    zhop(1, 3, 0)
    zhop(-1, 3, 1)
    lwait("z")
    lsend("x")
    text(2)
    add_core(2)
    add_core(6)
    zhop(1, 2, 1)
    zhop(-1, 2, 0)
    zhop(1, 2, 0)
    zhop(-1, 2, 1)
    text(1)
    add_core(1)
    add_core(7)
    zhop(1, 1, 1)
    zhop(-1, 1, 0)
    image(0)
    lwait("x")
    lsend("y")

    for k in (1, 3, 2):
        pa[k].wait_recv()
        pb[k].wait_recv()
        own[...] += decode(irecv[pl.ds((k - 1) * 256, 256), :])
    qa, qb = {}, {}
    for n, j in enumerate((2, 1, 3)):
        p2send[pl.ds(n * 64, HALF), :] = encode(own[pl.ds(j * HALF, HALF), :])
        p2send[pl.ds(n * 64 + HALF, HALF), :] = encode(own[pl.ds(128 + j * HALF, HALF), :])
        qa[j] = copy(p2send.at[pl.ds(n * 64, HALF)], p2recv.at[pl.ds(n * 64, HALF)], dev(dx=j))
        qb[j] = copy(p2send.at[pl.ds(n * 64 + HALF, HALF)], p2recv.at[pl.ds(n * 64 + HALF, HALF)], dev(dy=j))
        qa[j].start()
        qb[j].start()
    zhop(1, 1, 0)
    zhop(-1, 1, 1)

    def restore(ref, grads):
        values = ref[...].astype(F32)
        inverse = lax.rsqrt(jnp.sum(values * values, axis=1, keepdims=True) + 1e-06)
        inner = jnp.sum(values * grads, axis=1, keepdims=True)
        return inverse * grads - inverse * inverse * inverse * values * inner

    p2[pl.ds(0, HALF), :] = own[pl.ds(0, HALF), :]
    p2[pl.ds(HALF, HALF), :] = own[pl.ds(128, HALF), :]
    for n, j in enumerate((2, 1, 3)):
        qa[j].wait_recv()
        qb[j].wait_recv()
        p2[...] += decode(p2recv[pl.ds(n * 64, 64), :])
    gx_ref[...] = restore(x_ref, scale * p2[...])

    lwait("y")
    loss_ref[0] = lsum[0, 0] / 16384.0

    for h in (0, 1):
        for direction in (1, -1):
            zc[direction, 1, h].wait_recv()
            r = zslots[direction, 1, h]
            tf[pl.ds(h * HALF, HALF), :] += decode(zrecv[pl.ds(r, HALF), :])
    gy_ref[...] = restore(y_ref, scale * tf[pl.ds(0, ROWS), :])
    for c in started:
        c.wait_send()


COPIES = 120


def local(picture_embeddings, caption_embeddings, sharpness_factor, pairing_shift):
    vmem = pl.BlockSpec(memory_space=pltpu.VMEM)
    smem = pl.BlockSpec(memory_space=pltpu.SMEM)
    return pl.pallas_call(
        kernel,
        out_shape=(
            jax.ShapeDtypeStruct((1,), F32),
            jax.ShapeDtypeStruct((ROWS, D), F32),
            jax.ShapeDtypeStruct((ROWS, D), F32),
        ),
        in_specs=[vmem, vmem, smem, smem],
        out_specs=(smem, vmem, vmem),
        scratch_shapes=[
            pltpu.VMEM((1024, D), BF16),
            pltpu.VMEM((1024, D), BF16),
            pltpu.VMEM((1024, 1024), BF16),
            pltpu.VMEM((256, D), F32),
            pltpu.VMEM((768, D), BF16),
            pltpu.VMEM((768, D), BF16),
            pltpu.VMEM((ROWS, D), F32),
            pltpu.VMEM((192, D), BF16),
            pltpu.VMEM((192, D), BF16),
            pltpu.VMEM((1024, D), F32),
            pltpu.VMEM((512, D), F32),
            pltpu.VMEM((14 * HALF, D), BF16),
            pltpu.VMEM((14 * HALF, D), BF16),
            pltpu.VMEM((8, 256), F32),
            pltpu.VMEM((8, 128), F32),
            pltpu.VMEM((18, 8, 128), F32),
            pltpu.SemaphoreType.DMA((COPIES,)),
            pltpu.SemaphoreType.DMA((COPIES,)),
        ],
        compiler_params=pltpu.CompilerParams(collective_id=0, has_side_effects=True, vmem_limit_bytes=56 * 2**20),
    )(picture_embeddings, caption_embeddings, sharpness_factor, pairing_shift)


def solution(mesh):
    in_specs = (P(("img", "txt"), None), P(("txt", "img"), None), P(), P())
    out_specs = (P(), P(("img", "txt"), None), P(("txt", "img"), None))
    return jax.shard_map(local, mesh=mesh, in_specs=in_specs, out_specs=out_specs, check_vma=False)
```

```python
import jax
import jax.numpy as jnp
from jax import lax
from jax.experimental import pallas as pl
from jax.experimental.pallas import tpu as pltpu
from jax.sharding import PartitionSpec as P

MESH = pl.DeviceIdType.MESH
F32 = jnp.float32
BF16 = jnp.bfloat16
ROWS = 64
HALF = 32
PIECE = 16
D = 1152
LOG2E = 1.4426950408889634
POS = {0: 0, 1: 1, 7: 2, 2: 3, 6: 4, 3: 5, 5: 6, 4: 7}
CHUNK = {0: 0, 1: 1, 3: 2, 2: 3}
RATE = {"core": 300.0}
LINK_RATE = 20.6
LATENCY = {"core": 0.8, 1: 2.0, 2: 2.7}
BACKLOG = 1.6
ISSUE = 0.03
WAIT = 0.015


class Schedule:
    def __init__(self):
        self.tasks = {}

    def op(self, name, cost, deps, fn):
        self.tasks[name] = dict(name=name, msg=False, cost=cost, deps=list(deps), fn=fn)

    def msg(self, name, links, rows, lat, deps, make, sent, come):
        took = max([rows / RATE.get(x, LINK_RATE) for x in links], default=0.0)
        self.tasks[name] = dict(name=name, msg=True, links=links, took=took, lat=lat, deps=list(deps), fn=make, sent=sent, come=come)

    def levels(self):
        users = {n: [] for n in self.tasks}
        for n, t in self.tasks.items():
            for d in t["deps"]:
                users[d].append(n)
        level = {}

        def visit(n):
            if n not in level:
                t = self.tasks[n]
                own = ISSUE + t["lat"] + t["took"] if t["msg"] else t["cost"]
                level[n] = own + max([visit(u) for u in users[n]], default=0.0)
            return level[n]

        for n in self.tasks:
            visit(n)
        return level

    def order(self):
        level = self.levels()
        now, arrived, free, out, waited = 0.0, {}, {}, [], set()
        left = list(self.tasks)
        self.times = {}
        while left:
            ready, later = [], []
            for n in left:
                t = self.tasks[n]
                if any(d not in arrived for d in t["deps"]):
                    continue
                at = max([arrived[d] for d in t["deps"]] + [free.get(x, 0.0) - BACKLOG for x in t.get("links", ())], default=0.0)
                if at <= now + 1e-9:
                    ready.append(n)
                else:
                    later.append(at)
            if not ready:
                now = min(later)
                continue
            n = max(ready, key=lambda n: (self.tasks[n]["msg"], level[n]))
            left.remove(n)
            out.append(n)
            t = self.tasks[n]
            for d in t["deps"]:
                if self.tasks[d]["msg"] and d not in waited:
                    waited.add(d)
                    now += WAIT
            if t["msg"]:
                now += ISSUE
                end = max([now] + [free.get(x, 0.0) for x in t["links"]]) + t["took"]
                for x in t["links"]:
                    free[x] = end
                arrived[n] = end + t["lat"]
            else:
                now += t["cost"]
                arrived[n] = now
            self.times[n] = now
        return out

    def emit(self, ssem, rsem, sizes):
        number = {True: {}, False: {}}
        members = {}
        for n, t in self.tasks.items():
            if t["msg"]:
                number[True].setdefault(t["sent"], len(number[True]))
                number[False].setdefault(t["come"], len(number[False]))
                members.setdefault(t["come"], []).append(n)
        assert len(number[True]) <= SENT and len(number[False]) <= COME, "semaphores"
        copies, received = {}, set()

        def wait_group(sem, ref):
            pltpu.make_async_copy(ref, ref, sem).wait()

        def receive(come):
            if come in received:
                return
            received.add(come)
            assert all(m in copies for m in members[come]), "group"
            if len(members[come]) == 1:
                copies[members[come][0]].wait_recv()
            else:
                wait_group(rsem.at[number[False][come]], sizes[come])

        for n in self.order():
            t = self.tasks[n]
            for d in t["deps"]:
                if self.tasks[d]["msg"]:
                    receive(self.tasks[d]["come"])
            if t["msg"]:
                copies[n] = t["fn"](ssem.at[number[True][t["sent"]]], rsem.at[number[False][t["come"]]])
                copies[n].start()
            else:
                t["fn"]()
        for come in members:
            receive(come)
        for sent, i in number[True].items():
            wait_group(ssem.at[i], sizes[sent])


def encode(v):
    return (v * jnp.abs(v)).astype(BF16)


def decode(u):
    u = u.astype(F32)
    return u * lax.rsqrt(jnp.maximum(jnp.abs(u), 1e-37))


def log1p(p):
    small = p * (1.0 - p * (0.5 - p * (1.0 / 3.0 - p * 0.25)))
    return jnp.where(p < 0.01, small, jnp.log(1.0 + p))


def kernel(x_ref, y_ref, scale_ref, shift_ref, out_ref,
           xg, yg, w, imf, isend, irecv, p2send, p2recv, tf, crecv, zsend, zrecv,
           lacc, lsum, lrecv, ssem, rsem):
    img, txt = lax.axis_index("img"), lax.axis_index("txt")
    Y, C = img // 2, img % 2
    X, Z = txt // 8, txt % 8

    def dev(dx=0, dy=0, dz=0, dc=0):
        return (((Y + dy) % 4) * 2 + (C + dc) % 2, ((X + dx) % 4) * 8 + (Z + dz) % 8)

    barrier = pltpu.get_barrier_semaphore()
    peers = ([dev(dz=i) for i in range(1, 8)] + [dev(dx=i) for i in (1, 2, 3)] + [dev(dy=i) for i in (1, 2, 3)]
             + [dev(dc=1)])
    for p in peers:
        pl.semaphore_signal(barrier, inc=1, device_id=p, device_id_type=MESH)

    def unit(ref):
        values = ref[...].astype(F32)
        inverse = lax.rsqrt(jnp.sum(values * values, axis=1, keepdims=True) + 1e-06)
        return (values * inverse).astype(BF16)

    def A(k, j):
        return CHUNK[k] * 256 + j * HALF

    def B(k, j):
        return CHUNK[k] * 256 + 128 + j * HALF

    def yrow(s, rc):
        return POS[s] * 128 + rc * ROWS

    scale = scale_ref[0]
    shift = shift_ref[0]

    g = Schedule()

    def send(name, links, rows, deps, src, dst, to, sent, come=None, lat=None):
        if lat is None:
            lat = LATENCY["core"] if links == ["core"] else LATENCY[len(links)]
        g.msg(name, links, rows, lat, deps, lambda ss, rs: pltpu.make_async_remote_copy(
            src_ref=src, dst_ref=dst, send_sem=ss, recv_sem=rs, device_id=to, device_id_type=MESH), sent, come or name)

    def own_text():
        yg[pl.ds(yrow(0, 0), ROWS)] = unit(y_ref)
        pl.semaphore_wait(barrier, len(peers))

    def own_image():
        xn = unit(x_ref)
        xg[pl.ds(A(0, 0), HALF)] = xn[:HALF]
        xg[pl.ds(B(0, 0), HALF)] = xn[HALF:]
        lacc[...] = jnp.zeros_like(lacc)

    g.op("ny", 0.3, [], own_text)
    g.op("nx", 0.3, ["ny"], own_image)

    def rows_of(ref, start, n):
        return ref.at[pl.ds(start, n)]

    for t in (1, 2, 3, 4):
        for h in range(ROWS // PIECE):
            o = h * PIECE
            if t < 4 or o < HALF:
                send(f"u{t}{h}", ["z+"], PIECE, [f"u{t - 1}{h}"] if t > 1 else ["ny"],
                     rows_of(yg, yrow((9 - t) % 8, 0) + o, PIECE), rows_of(yg, yrow(8 - t, 0) + o, PIECE), dev(dz=1), "SY", "R4" if t == 4 else None)
            if t < 4 or o >= HALF:
                send(f"d{t}{h}", ["z-"], PIECE, [f"d{t - 1}{h}"] if t > 1 else ["ny"],
                     rows_of(yg, yrow(t - 1, 0) + o, PIECE), rows_of(yg, yrow(t, 0) + o, PIECE), dev(dz=-1), "SY", "R4" if t == 4 else None)
    pieces = range(ROWS // PIECE)
    yhave = {0: ["ny"], 4: [f"u4{h}" for h in pieces if h * PIECE < HALF] + [f"d4{h}" for h in pieces if h * PIECE >= HALF]}
    for t in (1, 2, 3):
        yhave[8 - t] = [f"u{t}{h}" for h in pieces]
        yhave[t] = [f"d{t}{h}" for h in pieces]
    for s in range(8):
        send(f"c{s}", ["core"], ROWS, yhave[s], rows_of(yg, yrow(s, 0), ROWS), rows_of(yg, yrow(s, 1), ROWS), dev(dc=1), "SC")

    def both(name, d, rows, da, db, a, a2, b, b2, n):
        links = {1: ["{}+"], 3: ["{}-"], 2: ["{}+", "{}-"]}[d % 4]
        first = name[0] == "f"
        come = "RT" if name[0] == "t" else "R" + name
        ax, bx = ("x", "y") if first else ("y", "x")
        send(name + "a", [x.format(ax) for x in links], rows, da, rows_of(xg, a, n), rows_of(xg, a2, n), dev(**{"d" + ax: d}), "SX", come)
        send(name + "b", [x.format(bx) for x in links], rows, db, rows_of(xg, b, n), rows_of(xg, b2, n), dev(**{"d" + bx: d}), "SX", come)

    for j, d in ((3, 1), (1, -1), (2, 2)):
        both(f"f{j}", d, HALF, ["nx"], ["nx"], A(0, 0), A(0, j), B(0, 0), B(0, j), HALF)
    for j in range(4):
        for k, d in ((3, 1), (1, -1)):
            da = db = [f"f{j}a", f"f{j}b"] if j else ["nx"]
            both(f"s{k}{j}", d, HALF, da, db, A(0, j), A(k, j), B(0, j), B(k, j), HALF)
            o = 16 if k == 3 else 0
            both(f"t{k}{j}", d, 16, [f"s{k}{j}a", f"s{k}{j}b"], [f"s{k}{j}a", f"s{k}{j}b"], A(k, j) + o, A(2, j) + o, B(k, j) + o, B(2, j) + o, 16)
    xhave = {0: [f"f{j}{q}" for j in (1, 2, 3) for q in "ab"], 2: [f"t{k}{j}{q}" for k in (1, 3) for j in range(4) for q in "ab"]}
    for k in (1, 3):
        xhave[k] = [f"s{k}{j}{q}" for j in range(4) for q in "ab"]

    def tile(r0, nr, c0, nc):
        def run():
            dots = lax.dot_general(xg[pl.ds(r0, nr), :], yg[pl.ds(c0, nc), :], (((1,), (1,)), ((), ())),
                                   preferred_element_type=F32)
            e = jnp.exp2(dots * (scale * LOG2E) + shift * LOG2E)
            d = 1.0 + e
            r = pl.reciprocal(d, approx=True)
            r = r * (2.0 - d * r)
            w[pl.ds(r0, nr), pl.ds(c0, nc)] = (e * r).astype(BF16)
            m = nr // 8
            n = m // 3
            e, d = e.reshape(m, 8, nc), d.reshape(m, 8, nc)
            p = e[:n] * d[n : 2 * n] + e[n : 2 * n]
            p = p * d[2 * n : 3 * n] + e[2 * n : 3 * n]
            total = jnp.sum(log1p(p), axis=0)
            if m - 3 * n == 2:
                total += log1p(e[m - 2] * d[m - 1] + e[m - 1])
            elif m - 3 * n == 1:
                total += log1p(e[m - 1])
            for c in range(0, nc, 128):
                lacc[...] += total[:, c : c + 128]

        return run

    groups = {"a": (0, 384, (0, 1, 7)), "b": (384, 256, (2, 6)), "c": (640, 256, (3, 5)), "d": (896, 128, (4,))}
    tiles = []

    def add_tile(chunks, cols, cost):
        r0 = min(CHUNK[k] for k in chunks) * 256
        c0 = min(groups[c][0] for c in cols)
        nc = sum(groups[c][1] for c in cols)
        deps = sum([xhave[k] for k in chunks], [])
        for c in cols:
            for s in groups[c][2]:
                deps = deps + yhave[s] + [f"c{s}"]
        tiles.append("w" + "".join(map(str, chunks)) + cols)
        g.op(tiles[-1], cost, deps, tile(r0, 256 * len(chunks), c0, nc))

    add_tile((0,), "a", 0.58)
    add_tile((0,), "b", 0.44)
    add_tile((0,), "c", 0.44)
    add_tile((1, 3), "a", 1.0)
    add_tile((1, 3), "b", 0.72)
    add_tile((1, 3), "c", 0.72)
    add_tile((2,), "abcd", 1.3)
    add_tile((0, 1, 3), "d", 0.6)

    def positive(place, h, k, j, xx):
        rc = (Z + C) % 2
        row = pl.multiple_of(place * 256 + h * 128 + j * HALF, HALF)
        s = (4 * C + xx - Z + 8) % 8
        pos = jnp.where(s == 0, 0, jnp.where(s == 4, 7, jnp.where(s < 4, 2 * s - 1, 2 * (8 - s))))
        col = pl.multiple_of(pos * 128, 128)
        yr = pl.multiple_of(pos * 128 + rc * ROWS + h * HALF, HALF)
        xv = xg[pl.ds(row, HALF), :].astype(F32)
        yv = yg[pl.ds(yr, HALF), :].astype(F32)
        z = scale * jnp.sum(xv * yv, axis=1, keepdims=True) + shift
        e = jnp.exp(z)
        wd = (e / (1.0 + e) - 1.0).astype(BF16)
        lane = lax.broadcasted_iota(jnp.int32, (HALF, 128), 1)
        sub = lax.broadcasted_iota(jnp.int32, (HALF, 128), 0)
        hit = lane == sub + rc * ROWS + h * HALF
        old = w[pl.ds(row, HALF), pl.ds(col, 128)]
        w[pl.ds(row, HALF), pl.ds(col, 128)] = jnp.where(hit, wd.astype(F32), old.astype(F32)).astype(BF16)
        zz = jnp.where(hit, z, 0.0)
        lacc[...] -= jnp.sum(zz.reshape(4, 8, 128), axis=0)

    def positives(k):
        def run():
            @pl.when(Y == Z // 2)
            def _():
                positive(CHUNK[k], 1, k, (X - Y + 4) % 4, (X + k) % 4)

                @pl.when((X - Y + 4) % 4 == k)
                def _():
                    for xx in range(4):
                        positive(CHUNK[k], 0, k, (xx - X + 4) % 4, xx)

        return run

    for k in range(4):
        g.op(f"pos{k}", 0.15, [n for n in tiles if str(k) in n], positives(k))
    fixed = [f"pos{k}" for k in range(4)]

    def loss_axis(axis, before):
        n, me, base, kw, lat = {"c": (2, C, 0, "dc", 0.8), "z": (8, Z, 2, "dz", 4.0), "x": (4, X, 10, "dx", 2.6),
                                "y": (4, Y, 14, "dy", 2.6)}[axis]

        def run():
            if before is None:
                v = jnp.full((8, 128), jnp.sum(lacc[...]), F32)
            else:
                b, m = before
                v = lrecv[b]
                for o in range(1, m):
                    v = v + lrecv[b + o]
            lrecv[base + me] = v

        prev = {"c": "", "z": "c", "x": "z", "y": "x"}[axis]
        deps = fixed if axis == "c" else ["l" + prev] + [f"l{prev}{o}" for o in range(1, {"c": 2, "z": 8, "x": 4}[prev])]
        g.op("l" + axis, 0.1, deps, run)
        for o in range(1, n):
            send(f"l{axis}{o}", [], 0, ["l" + axis], lrecv.at[base + me], lrecv.at[base + me], dev(**{kw: o}), "SL", "RL" + axis, lat)

    loss_axis("c", None)
    loss_axis("z", (0, 2))
    loss_axis("x", (2, 8))
    loss_axis("y", (10, 4))

    def loss_end():
        v = lrecv[14]
        for o in range(1, 4):
            v = v + lrecv[14 + o]
        lsum[...] = v
        out_ref[pl.ds(2 * ROWS, 8), pl.ds(0, 128)] = lsum[...] * (1.0 / 16384.0)

    g.op("loss", 0.1, ["ly"] + [f"ly{o}" for o in (1, 2, 3)], loss_end)

    def text(c0, nc):
        def run():
            tf[pl.ds(c0, nc), :] = lax.dot_general(w[:, pl.ds(c0, nc)], xg[...], (((0,), (0,)), ((), ())),
                                                   preferred_element_type=F32)

        return run

    for n, c0, nc, slots in (("4", 896, 128, (4,)), ("35", 640, 256, (3, 5)), ("26", 384, 256, (2, 6)),
                             ("17", 128, 256, (1, 7)), ("0", 0, 128, (0,))):
        g.op("x" + n, 0.06 + 0.52 * nc / 256, fixed, text(c0, nc))
        for s in slots:
            send(f"x{n}c{s}", ["core"], 2 * ROWS, ["x" + n], rows_of(tf, yrow(s, 1), ROWS), rows_of(crecv, s * ROWS, ROWS), dev(dc=1), "SK")

            def add(s=s):
                tf[pl.ds(yrow(s, 0), ROWS), :] += crecv[pl.ds(s * ROWS, ROWS), :]

            g.op(f"k{s}", 0.07, ["x" + n, f"x{n}c{s}"], add)

    slot = 0
    for sign, q in ((1, "p"), (-1, "m")):
        for h in pieces:
            first = 4 if (sign > 0) == (h * PIECE < HALF) else 3
            for t in range(first, 0, -1):
                s = t if sign > 0 else 8 - t
                deps = [f"k{s}"] + ([f"z{q}{t + 1}{h}"] if t < first else [])
                r = slot * PIECE

                def hop(s=s, h=h, r=r, more=t < first):
                    v = tf[pl.ds(yrow(s, 0) + h * PIECE, PIECE), :]
                    if more:
                        v = v + decode(zrecv[pl.ds(r - PIECE, PIECE), :])
                    zsend[pl.ds(r, PIECE), :] = encode(v)

                g.op(f"h{q}{t}{h}", 0.04 + 0.0014 * PIECE, deps, hop)
                send(f"z{q}{t}{h}", ["z+" if sign > 0 else "z-"], PIECE, [f"h{q}{t}{h}"], rows_of(zsend, r, PIECE), rows_of(zrecv, r, PIECE), dev(dz=sign), "SZ")
                slot += 1

            def last(h=h, r=r):
                tf[pl.ds(yrow(0, 0) + h * PIECE, PIECE), :] += decode(zrecv[pl.ds(r, PIECE), :])

            g.op(f"e{q}{h}", 0.06, ["k0", f"z{q}1{h}"], last)

    def text_end():
        out_ref[pl.ds(ROWS, ROWS), :] = scale * tf[pl.ds(yrow(0, 0), ROWS), :]

    g.op("gy", 0.3, [f"e{q}{h}" for q in "pm" for h in pieces], text_end)

    def image(k):
        def run():
            part = jnp.dot(w[pl.ds(CHUNK[k] * 256, 256), :], yg[...], preferred_element_type=F32)
            if k == 2:
                isend[pl.ds(0, 256), :] = encode(part)
                return
            imf[pl.ds(CHUNK[k] * 256, 256), :] = part
            if k:
                for b in (0, 128):
                    o = CHUNK[k] * 256 + b + (64 if k == 1 else 0)
                    isend[pl.ds(o, 64), :] = encode(imf[pl.ds(o, 64), :])

        return run

    for k in (0, 1, 2, 3):
        g.op(f"i{k}", 0.7, [f"pos{k}"], image(k))
    for q, b, ax in (("a", 0, "y"), ("b", 128, "x")):
        def part(name, start, deps, d, b=b, ax=ax, q=q):
            send(name + q, [ax + ("+" if d > 0 else "-")], HALF, deps, rows_of(isend, start + b, HALF), rows_of(irecv, start + b, HALF),
                 dev(**{"d" + ax: d}), "SI")

        ox = "x" if q == "a" else "y"
        for j in (1, 2, 0, 3):
            near, far, d = (1, 3, 1) if j in (0, 1) else (3, 1, -1)
            o2, on, of = j * HALF, CHUNK[near] * 256 + j * HALF, CHUNK[far] * 256 + j * HALF
            part(f"m2{j}", o2, ["i2"], d)
            part(f"m{far}{j}", of, [f"i{far}"], -d)

            def join(on=on, o2=o2, b=b):
                v = imf[pl.ds(on + b, HALF), :] + decode(irecv[pl.ds(o2 + b, HALF), :])
                isend[pl.ds(on + b, HALF), :] = encode(v)

            g.op(f"j{j}{q}", 0.1, [f"i{near}", f"m2{j}{q}"], join)
            part(f"m{near}{j}", on, [f"j{j}{q}"], d)
            r = (2 * (j - 1) + b // 128) * HALF

            def add_up(j=j, b=b, on=on, of=of, r=r):
                v = imf[pl.ds(b + j * HALF, HALF), :] + decode(irecv[pl.ds(on + b, HALF), :]) + decode(irecv[pl.ds(of + b, HALF), :])
                if j:
                    p2send[pl.ds(r, HALF), :] = encode(v)
                else:
                    imf[pl.ds(b, HALF), :] = v

            g.op(f"a{j}{q}", 0.12, ["i0", f"m{near}{j}{q}", f"m{far}{j}{q}"], add_up)
            if j:
                links = {1: [ox + "+"], 2: [ox + "+", ox + "-"], 3: [ox + "-"]}[j]
                send(f"n{j}{q}", links, HALF, [f"a{j}{q}"], rows_of(p2send, r, HALF), rows_of(p2recv, r, HALF), dev(**{"d" + ox: j}), "SN")

                def gather_up(j=j, b=b, r=r):
                    imf[pl.ds(b, HALF), :] += decode(p2recv[pl.ds(r, HALF), :])

                g.op(f"o{j}{q}", 0.07, ["a0" + q, f"n{j}{q}"], gather_up)

    def image_end():
        out_ref[pl.ds(0, HALF), :] = scale * imf[pl.ds(0, HALF), :]
        out_ref[pl.ds(HALF, HALF), :] = scale * imf[pl.ds(128, HALF), :]

    g.op("gx", 0.4, [f"o{j}{q}" for j in (1, 2, 3) for q in "ab"], image_end)
    sizes = {"SY": zsend, "SC": rows_of(xg, 0, 512), "SX": rows_of(xg, 0, 960), "SL": rows_of(lrecv, 0, 14), "SK": crecv, "SZ": zsend,
             "SI": isend, "SN": p2send, "R4": rows_of(xg, 0, 64), "RT": rows_of(xg, 0, 256), "RLc": lrecv.at[0],
             "RLz": rows_of(lrecv, 0, 7), "RLx": rows_of(lrecv, 0, 3), "RLy": rows_of(lrecv, 0, 3)}
    for n, t in g.tasks.items():
        if t["msg"] and t["come"] not in sizes:
            sizes[t["come"]] = rows_of(xg, 0, 64)
    g.emit(ssem, rsem, sizes)


def restore(ref, grads):
    values = ref[...].astype(F32)
    inverse = lax.rsqrt(jnp.sum(values * values, axis=1, keepdims=True) + 1e-06)
    inner = jnp.sum(values * grads, axis=1, keepdims=True)
    return inverse * grads - inverse * inverse * inverse * values * inner


def finish(sums_ref, x_ref, y_ref, loss_ref, gx_ref, gy_ref):
    gx_ref[...] = restore(x_ref, sums_ref[pl.ds(0, ROWS), :])
    gy_ref[...] = restore(y_ref, sums_ref[pl.ds(ROWS, ROWS), :])
    loss_ref[0] = sums_ref[2 * ROWS, 0]


SENT = 8
COME = 117


def local(picture_embeddings, caption_embeddings, sharpness_factor, pairing_shift):
    vmem = pl.BlockSpec(memory_space=pltpu.VMEM)
    smem = pl.BlockSpec(memory_space=pltpu.SMEM)
    sums = pl.pallas_call(
        kernel,
        out_shape=jax.ShapeDtypeStruct((2 * ROWS + 8, D), F32),
        in_specs=[vmem, vmem, smem, smem],
        out_specs=vmem,
        scratch_shapes=[
            pltpu.VMEM((1024, D), BF16),
            pltpu.VMEM((1024, D), BF16),
            pltpu.VMEM((1024, 1024), BF16),
            pltpu.VMEM((768, D), F32),
            pltpu.VMEM((768, D), BF16),
            pltpu.VMEM((768, D), BF16),
            pltpu.VMEM((192, D), BF16),
            pltpu.VMEM((192, D), BF16),
            pltpu.VMEM((1024, D), F32),
            pltpu.VMEM((512, D), F32),
            pltpu.VMEM((448, D), BF16),
            pltpu.VMEM((448, D), BF16),
            pltpu.VMEM((8, 128), F32),
            pltpu.VMEM((8, 128), F32),
            pltpu.VMEM((18, 8, 128), F32),
            pltpu.SemaphoreType.DMA((SENT,)),
            pltpu.SemaphoreType.DMA((COME,)),
        ],
        compiler_params=pltpu.CompilerParams(collective_id=0, has_side_effects=True, vmem_limit_bytes=56 * 2**20),
    )(picture_embeddings, caption_embeddings, sharpness_factor, pairing_shift)
    return pl.pallas_call(
        finish,
        out_shape=(
            jax.ShapeDtypeStruct((1,), F32),
            jax.ShapeDtypeStruct((ROWS, D), F32),
            jax.ShapeDtypeStruct((ROWS, D), F32),
        ),
        in_specs=[vmem, vmem, vmem],
        out_specs=(smem, vmem, vmem),
    )(sums, picture_embeddings, caption_embeddings)


def solution(mesh):
    in_specs = (P(("img", "txt"), None), P(("txt", "img"), None), P(), P())
    out_specs = (P(), P(("img", "txt"), None), P(("txt", "img"), None))
    return jax.shard_map(local, mesh=mesh, in_specs=in_specs, out_specs=out_specs, check_vma=False)
```

```python
import jax
import jax.numpy as jnp
from jax import lax
from jax.experimental import pallas as pl
from jax.experimental.pallas import tpu as pltpu
from jax.sharding import PartitionSpec as P

MESH = pl.DeviceIdType.MESH
F32 = jnp.float32
BF16 = jnp.bfloat16
ROWS = 64
HALF = 32
PIECE = 16
D = 1152
LOG2E = 1.4426950408889634
POS = {0: 0, 1: 1, 7: 2, 2: 3, 6: 4, 3: 5, 5: 6, 4: 7}
CHUNK = {0: 0, 1: 1, 3: 2, 2: 3}
RATE = {"core": 300.0}
LINK_RATE = 20.6
LATENCY = {"core": 0.8, 1: 2.0, 2: 2.7}
BACKLOG = 1.6
ISSUE = 0.03
WAIT = 0.015


class Schedule:
    def __init__(self):
        self.tasks = {}

    def op(self, name, cost, deps, fn):
        self.tasks[name] = dict(name=name, msg=False, cost=cost, deps=list(deps), fn=fn)

    def msg(self, name, links, rows, lat, deps, make, sent, come):
        took = max([rows / RATE.get(x, LINK_RATE) for x in links], default=0.0)
        self.tasks[name] = dict(name=name, msg=True, links=links, took=took, lat=lat, deps=list(deps), fn=make, sent=sent, come=come)

    def levels(self):
        users = {n: [] for n in self.tasks}
        for n, t in self.tasks.items():
            for d in t["deps"]:
                users[d].append(n)
        level = {}

        def visit(n):
            if n not in level:
                t = self.tasks[n]
                own = ISSUE + t["lat"] + t["took"] if t["msg"] else t["cost"]
                level[n] = own + max([visit(u) for u in users[n]], default=0.0)
            return level[n]

        for n in self.tasks:
            visit(n)
        return level

    def order(self):
        level = self.levels()
        now, arrived, free, out, waited = 0.0, {}, {}, [], set()
        left = list(self.tasks)
        self.times = {}
        while left:
            ready, later = [], []
            for n in left:
                t = self.tasks[n]
                if any(d not in arrived for d in t["deps"]):
                    continue
                at = max([arrived[d] for d in t["deps"]] + [free.get(x, 0.0) - BACKLOG for x in t.get("links", ())], default=0.0)
                if at <= now + 1e-9:
                    ready.append(n)
                else:
                    later.append(at)
            if not ready:
                now = min(later)
                continue
            n = max(ready, key=lambda n: (self.tasks[n]["msg"], level[n]))
            left.remove(n)
            out.append(n)
            t = self.tasks[n]
            for d in t["deps"]:
                if self.tasks[d]["msg"] and d not in waited:
                    waited.add(d)
                    now += WAIT
            if t["msg"]:
                now += ISSUE
                end = max([now] + [free.get(x, 0.0) for x in t["links"]]) + t["took"]
                for x in t["links"]:
                    free[x] = end
                arrived[n] = end + t["lat"]
            else:
                now += t["cost"]
                arrived[n] = now
            self.times[n] = now
        return out

    def emit(self, ssem, rsem, sizes):
        number = {True: {}, False: {}}
        members = {}
        for n, t in self.tasks.items():
            if t["msg"]:
                number[True].setdefault(t["sent"], len(number[True]))
                number[False].setdefault(t["come"], len(number[False]))
                members.setdefault(t["come"], []).append(n)
        assert len(number[True]) <= SENT and len(number[False]) <= COME, "semaphores"
        copies, received = {}, set()

        def wait_group(sem, ref):
            pltpu.make_async_copy(ref, ref, sem).wait()

        def receive(come):
            if come in received:
                return
            received.add(come)
            assert all(m in copies for m in members[come]), "group"
            if len(members[come]) == 1:
                copies[members[come][0]].wait_recv()
            else:
                wait_group(rsem.at[number[False][come]], sizes[come])

        for n in self.order():
            t = self.tasks[n]
            for d in t["deps"]:
                if self.tasks[d]["msg"]:
                    receive(self.tasks[d]["come"])
            if t["msg"]:
                copies[n] = t["fn"](ssem.at[number[True][t["sent"]]], rsem.at[number[False][t["come"]]])
                copies[n].start()
            else:
                t["fn"]()
        for come in members:
            receive(come)
        for sent, i in number[True].items():
            wait_group(ssem.at[i], sizes[sent])


def encode(v):
    return (v * jnp.abs(v)).astype(BF16)


def decode(u):
    u = u.astype(F32)
    return u * lax.rsqrt(jnp.maximum(jnp.abs(u), 1e-37))


def log1p(p):
    small = p * (1.0 - p * (0.5 - p * (1.0 / 3.0 - p * 0.25)))
    return jnp.where(p < 0.01, small, jnp.log(1.0 + p))


def restore(raw, grads):
    values = raw.astype(F32)
    inverse = lax.rsqrt(jnp.sum(values * values, axis=1, keepdims=True) + 1e-06)
    inner = jnp.sum(values * grads, axis=1, keepdims=True)
    return inverse * grads - inverse * inverse * inverse * values * inner


def kernel(x_hbm, y_hbm, scale_hbm, shift_hbm, out_ref,
           xg, yg, w, imf, isend, irecv, p2send, p2recv, tf, crecv, zsend, zrecv,
           lacc, lsum, lrecv, x_ref, y_ref, scale_ref, shift_ref, csem, ssem, rsem):
    img, txt = lax.axis_index("img"), lax.axis_index("txt")
    Y, C = img // 2, img % 2
    X, Z = txt // 8, txt % 8

    def dev(dx=0, dy=0, dz=0, dc=0):
        return (((Y + dy) % 4) * 2 + (C + dc) % 2, ((X + dx) % 4) * 8 + (Z + dz) % 8)

    inputs = [pltpu.make_async_copy(a, b, csem.at[i]) for i, (a, b) in enumerate(
        ((y_hbm, y_ref), (x_hbm, x_ref), (scale_hbm, scale_ref), (shift_hbm, shift_ref)))]
    for c in inputs:
        c.start()
    barrier = pltpu.get_barrier_semaphore()
    peers = ([dev(dz=1), dev(dz=-1)] + [dev(dx=i) for i in (1, 2, 3)] + [dev(dy=i) for i in (1, 2, 3)]
             + [dev(dc=1)])
    for p in peers:
        pl.semaphore_signal(barrier, inc=1, device_id=p, device_id_type=MESH)

    def unit(ref):
        values = ref[...].astype(F32)
        inverse = lax.rsqrt(jnp.sum(values * values, axis=1, keepdims=True) + 1e-06)
        return (values * inverse).astype(BF16)

    def A(k, j):
        return CHUNK[k] * 256 + j * HALF

    def B(k, j):
        return CHUNK[k] * 256 + 128 + j * HALF

    def yrow(s, rc):
        return POS[s] * 128 + rc * ROWS

    g = Schedule()

    def send(name, links, rows, deps, src, dst, to, sent, come=None, lat=None):
        if lat is None:
            lat = LATENCY["core"] if links == ["core"] else LATENCY[max(1, len(links))]
        g.msg(name, links, rows, lat, deps, lambda ss, rs: pltpu.make_async_remote_copy(
            src_ref=src, dst_ref=dst, send_sem=ss, recv_sem=rs, device_id=to, device_id_type=MESH), sent, come or name)

    def own_text():
        inputs[0].wait()
        yg[pl.ds(yrow(0, 0), ROWS)] = unit(y_ref)
        pl.semaphore_wait(barrier, len(peers))

    def own_image():
        inputs[1].wait()
        xn = unit(x_ref)
        xg[pl.ds(A(0, 0), HALF)] = xn[:HALF]
        xg[pl.ds(B(0, 0), HALF)] = xn[HALF:]
        lacc[...] = jnp.zeros_like(lacc)
        for c in inputs[2:]:
            c.wait()

    g.op("ny", 0.3, [], own_text)
    g.op("nx", 0.3, ["ny"], own_image)

    def rows_of(ref, start, n):
        return ref.at[pl.ds(start, n)]

    for t in (1, 2, 3, 4):
        for h in range(ROWS // PIECE):
            o = h * PIECE
            if t < 4 or o < HALF:
                send(f"u{t}{h}", ["z+"], PIECE, [f"u{t - 1}{h}"] if t > 1 else ["ny"],
                     rows_of(yg, yrow((9 - t) % 8, 0) + o, PIECE), rows_of(yg, yrow(8 - t, 0) + o, PIECE), dev(dz=1), "SY", "R4" if t == 4 else None)
            if t < 4 or o >= HALF:
                send(f"d{t}{h}", ["z-"], PIECE, [f"d{t - 1}{h}"] if t > 1 else ["ny"],
                     rows_of(yg, yrow(t - 1, 0) + o, PIECE), rows_of(yg, yrow(t, 0) + o, PIECE), dev(dz=-1), "SY", "R4" if t == 4 else None)
    pieces = range(ROWS // PIECE)
    yhave = {0: ["ny"], 4: [f"u4{h}" for h in pieces if h * PIECE < HALF] + [f"d4{h}" for h in pieces if h * PIECE >= HALF]}
    for t in (1, 2, 3):
        yhave[8 - t] = [f"u{t}{h}" for h in pieces]
        yhave[t] = [f"d{t}{h}" for h in pieces]
    for s in range(8):
        send(f"c{s}", ["core"], ROWS, yhave[s], rows_of(yg, yrow(s, 0), ROWS), rows_of(yg, yrow(s, 1), ROWS), dev(dc=1), "SC")

    def both(name, d, rows, da, db, a, a2, b, b2, n):
        links = {1: ["{}+"], 3: ["{}-"], 2: ["{}+", "{}-"]}[d % 4]
        first = name[0] == "f"
        come = "RT" if name[0] == "t" else "R" + name
        ax, bx = ("x", "y") if first else ("y", "x")
        send(name + "a", [x.format(ax) for x in links], rows, da, rows_of(xg, a, n), rows_of(xg, a2, n), dev(**{"d" + ax: d}), "SX", come)
        send(name + "b", [x.format(bx) for x in links], rows, db, rows_of(xg, b, n), rows_of(xg, b2, n), dev(**{"d" + bx: d}), "SX", come)

    for j, d in ((3, 1), (1, -1), (2, 2)):
        both(f"f{j}", d, HALF, ["nx"], ["nx"], A(0, 0), A(0, j), B(0, 0), B(0, j), HALF)
    for j in range(4):
        for k, d in ((3, 1), (1, -1)):
            da = db = [f"f{j}a", f"f{j}b"] if j else ["nx"]
            both(f"s{k}{j}", d, HALF, da, db, A(0, j), A(k, j), B(0, j), B(k, j), HALF)
            o = 16 if k == 3 else 0
            both(f"t{k}{j}", d, 16, [f"s{k}{j}a", f"s{k}{j}b"], [f"s{k}{j}a", f"s{k}{j}b"], A(k, j) + o, A(2, j) + o, B(k, j) + o, B(2, j) + o, 16)
    xhave = {0: [f"f{j}{q}" for j in (1, 2, 3) for q in "ab"], 2: [f"t{k}{j}{q}" for k in (1, 3) for j in range(4) for q in "ab"]}
    for k in (1, 3):
        xhave[k] = [f"s{k}{j}{q}" for j in range(4) for q in "ab"]

    def tile(r0, nr, c0, nc):
        def run():
            dots = lax.dot_general(xg[pl.ds(r0, nr), :], yg[pl.ds(c0, nc), :], (((1,), (1,)), ((), ())),
                                   preferred_element_type=F32)
            e = jnp.exp2(dots * (scale_ref[0] * LOG2E) + shift_ref[0] * LOG2E)
            d = 1.0 + e
            r = pl.reciprocal(d, approx=True)
            r = r * (2.0 - d * r)
            w[pl.ds(r0, nr), pl.ds(c0, nc)] = (e * r).astype(BF16)
            m = nr // 8
            n = m // 3
            e, d = e.reshape(m, 8, nc), d.reshape(m, 8, nc)
            p = e[:n] * d[n : 2 * n] + e[n : 2 * n]
            p = p * d[2 * n : 3 * n] + e[2 * n : 3 * n]
            total = jnp.sum(log1p(p), axis=0)
            if m - 3 * n == 2:
                total += log1p(e[m - 2] * d[m - 1] + e[m - 1])
            elif m - 3 * n == 1:
                total += log1p(e[m - 1])
            for c in range(0, nc, 128):
                lacc[...] += total[:, c : c + 128]

        return run

    groups = {"a": (0, 384, (0, 1, 7)), "b": (384, 256, (2, 6)), "c": (640, 256, (3, 5)), "d": (896, 128, (4,))}
    tiles = []

    def add_tile(chunks, cols, cost):
        r0 = min(CHUNK[k] for k in chunks) * 256
        c0 = min(groups[c][0] for c in cols)
        nc = sum(groups[c][1] for c in cols)
        deps = sum([xhave[k] for k in chunks], [])
        for c in cols:
            for s in groups[c][2]:
                deps = deps + yhave[s] + [f"c{s}"]
        tiles.append("w" + "".join(map(str, chunks)) + cols)
        g.op(tiles[-1], cost, deps, tile(r0, 256 * len(chunks), c0, nc))

    add_tile((0,), "a", 0.58)
    add_tile((0,), "b", 0.44)
    add_tile((0,), "c", 0.44)
    add_tile((1, 3), "a", 1.0)
    add_tile((1, 3), "b", 0.72)
    add_tile((1, 3), "c", 0.72)
    add_tile((2,), "abcd", 1.3)
    add_tile((0, 1, 3), "d", 0.6)

    def positive(place, h, k, j, xx):
        rc = (Z + C) % 2
        row = pl.multiple_of(place * 256 + h * 128 + j * HALF, HALF)
        s = (4 * C + xx - Z + 8) % 8
        pos = jnp.where(s == 0, 0, jnp.where(s == 4, 7, jnp.where(s < 4, 2 * s - 1, 2 * (8 - s))))
        col = pl.multiple_of(pos * 128, 128)
        yr = pl.multiple_of(pos * 128 + rc * ROWS + h * HALF, HALF)
        xv = xg[pl.ds(row, HALF), :].astype(F32)
        yv = yg[pl.ds(yr, HALF), :].astype(F32)
        z = scale_ref[0] * jnp.sum(xv * yv, axis=1, keepdims=True) + shift_ref[0]
        e = jnp.exp(z)
        wd = (e / (1.0 + e) - 1.0).astype(BF16)
        lane = lax.broadcasted_iota(jnp.int32, (HALF, 128), 1)
        sub = lax.broadcasted_iota(jnp.int32, (HALF, 128), 0)
        hit = lane == sub + rc * ROWS + h * HALF
        old = w[pl.ds(row, HALF), pl.ds(col, 128)]
        w[pl.ds(row, HALF), pl.ds(col, 128)] = jnp.where(hit, wd.astype(F32), old.astype(F32)).astype(BF16)
        zz = jnp.where(hit, z, 0.0)
        lacc[...] -= jnp.sum(zz.reshape(4, 8, 128), axis=0)

    def positives(k):
        def run():
            @pl.when(Y == Z // 2)
            def _():
                positive(CHUNK[k], 1, k, (X - Y + 4) % 4, (X + k) % 4)

                @pl.when((X - Y + 4) % 4 == k)
                def _():
                    for xx in range(4):
                        positive(CHUNK[k], 0, k, (xx - X + 4) % 4, xx)

        return run

    for k in range(4):
        g.op(f"pos{k}", 0.15, [n for n in tiles if str(k) in n], positives(k))
    fixed = [f"pos{k}" for k in range(4)]

    def loss_axis(axis, before):
        n, me, base, kw, lat = {"c": (2, C, 0, "dc", 0.8), "z": (8, Z, 2, "dz", 4.0), "x": (4, X, 10, "dx", 2.6),
                                "y": (4, Y, 14, "dy", 2.6)}[axis]

        def run():
            if before is None:
                v = jnp.full((8, 128), jnp.sum(lacc[...]), F32)
            else:
                b, m = before
                v = lrecv[b]
                for o in range(1, m):
                    v = v + lrecv[b + o]
            lrecv[base + me] = v

        prev = {"c": "", "z": "c", "x": "z", "y": "x"}[axis]
        hops = ("zu1", "zu2", "zu3", "zu4", "zd1", "zd2", "zd3")
        deps = fixed if axis == "c" else ["l" + prev] + ([f"l{q}" for q in hops] if prev == "z" else [f"l{prev}{o}" for o in range(1, {"c": 2, "x": 4}[prev])])
        g.op("l" + axis, 0.1, deps, run)
        if axis == "z":
            for q, sign, far in (("u", 1, 4), ("d", -1, 3)):
                for t in range(1, far + 1):
                    at = base + (Z - sign * (t - 1) + 8) % 8
                    send(f"lz{q}{t}", [], 0, [f"lz{q}{t - 1}" if t > 1 else "lz"], lrecv.at[at], lrecv.at[at], dev(dz=sign), "SL")
            return
        for o in range(1, n):
            send(f"l{axis}{o}", [], 0, ["l" + axis], lrecv.at[base + me], lrecv.at[base + me], dev(**{kw: o}), "SL", "RL" + axis, lat)

    loss_axis("c", None)
    loss_axis("z", (0, 2))
    loss_axis("x", (2, 8))
    loss_axis("y", (10, 4))

    def loss_end():
        v = lrecv[14]
        for o in range(1, 4):
            v = v + lrecv[14 + o]
        lsum[...] = v
        out_ref[pl.ds(2 * ROWS, 8), pl.ds(0, 128)] = lsum[...] * (1.0 / 16384.0)

    g.op("loss", 0.1, ["ly"] + [f"ly{o}" for o in (1, 2, 3)], loss_end)

    def text(c0, nc):
        def run():
            tf[pl.ds(c0, nc), :] = lax.dot_general(w[:, pl.ds(c0, nc)], xg[...], (((0,), (0,)), ((), ())),
                                                   preferred_element_type=F32)

        return run

    for n, c0, nc, slots in (("4", 896, 128, (4,)), ("35", 640, 256, (3, 5)), ("26", 384, 256, (2, 6)),
                             ("17", 128, 256, (1, 7)), ("0", 0, 128, (0,))):
        g.op("x" + n, 0.06 + 0.52 * nc / 256, fixed, text(c0, nc))
        for s in slots:
            send(f"x{n}c{s}", ["core"], 2 * ROWS, ["x" + n], rows_of(tf, yrow(s, 1), ROWS), rows_of(crecv, s * ROWS, ROWS), dev(dc=1), "SK")

            def add(s=s):
                tf[pl.ds(yrow(s, 0), ROWS), :] += crecv[pl.ds(s * ROWS, ROWS), :]

            g.op(f"k{s}", 0.07, ["x" + n, f"x{n}c{s}"], add)

    slot = 0
    for sign, q in ((1, "p"), (-1, "m")):
        for h in pieces:
            first = 4 if (sign > 0) == (h * PIECE < HALF) else 3
            for t in range(first, 0, -1):
                s = t if sign > 0 else 8 - t
                deps = [f"k{s}"] + ([f"z{q}{t + 1}{h}"] if t < first else [])
                r = slot * PIECE

                def hop(s=s, h=h, r=r, more=t < first):
                    v = tf[pl.ds(yrow(s, 0) + h * PIECE, PIECE), :]
                    if more:
                        v = v + decode(zrecv[pl.ds(r - PIECE, PIECE), :])
                    zsend[pl.ds(r, PIECE), :] = encode(v)

                g.op(f"h{q}{t}{h}", 0.04 + 0.0014 * PIECE, deps, hop)
                send(f"z{q}{t}{h}", ["z+" if sign > 0 else "z-"], PIECE, [f"h{q}{t}{h}"], rows_of(zsend, r, PIECE), rows_of(zrecv, r, PIECE), dev(dz=sign), "SZ")
                slot += 1

            def last(h=h, r=r):
                tf[pl.ds(yrow(0, 0) + h * PIECE, PIECE), :] += decode(zrecv[pl.ds(r, PIECE), :])

            g.op(f"e{q}{h}", 0.06, ["k0", f"z{q}1{h}"], last)

    def text_end():
        out_ref[pl.ds(ROWS, ROWS), :] = restore(y_ref[...], scale_ref[0] * tf[pl.ds(yrow(0, 0), ROWS), :])

    g.op("gy", 0.3, [f"e{q}{h}" for q in "pm" for h in pieces], text_end)

    def image(k):
        def run():
            part = jnp.dot(w[pl.ds(CHUNK[k] * 256, 256), :], yg[...], preferred_element_type=F32)
            if k == 2:
                isend[pl.ds(0, 256), :] = encode(part)
                return
            imf[pl.ds(CHUNK[k] * 256, 256), :] = part
            if k:
                for b in (0, 128):
                    o = CHUNK[k] * 256 + b + (64 if k == 1 else 0)
                    isend[pl.ds(o, 64), :] = encode(imf[pl.ds(o, 64), :])

        return run

    for k in (0, 1, 2, 3):
        g.op(f"i{k}", 0.7, [f"pos{k}"], image(k))
    for q, b, ax in (("a", 0, "y"), ("b", 128, "x")):
        def part(name, start, deps, d, b=b, ax=ax, q=q):
            send(name + q, [ax + ("+" if d > 0 else "-")], HALF, deps, rows_of(isend, start + b, HALF), rows_of(irecv, start + b, HALF),
                 dev(**{"d" + ax: d}), "SI")

        ox = "x" if q == "a" else "y"
        for j in (1, 2, 0, 3):
            near, far, d = (1, 3, 1) if j in (0, 1) else (3, 1, -1)
            o2, on, of = j * HALF, CHUNK[near] * 256 + j * HALF, CHUNK[far] * 256 + j * HALF
            part(f"m2{j}", o2, ["i2"], d)
            part(f"m{far}{j}", of, [f"i{far}"], -d)

            def join(on=on, o2=o2, b=b):
                v = imf[pl.ds(on + b, HALF), :] + decode(irecv[pl.ds(o2 + b, HALF), :])
                isend[pl.ds(on + b, HALF), :] = encode(v)

            g.op(f"j{j}{q}", 0.1, [f"i{near}", f"m2{j}{q}"], join)
            part(f"m{near}{j}", on, [f"j{j}{q}"], d)
            r = (2 * (j - 1) + b // 128) * HALF

            def add_up(j=j, b=b, on=on, of=of, r=r):
                v = imf[pl.ds(b + j * HALF, HALF), :] + decode(irecv[pl.ds(on + b, HALF), :]) + decode(irecv[pl.ds(of + b, HALF), :])
                if j:
                    p2send[pl.ds(r, HALF), :] = encode(v)
                else:
                    imf[pl.ds(b, HALF), :] = v

            g.op(f"a{j}{q}", 0.12, ["i0", f"m{near}{j}{q}", f"m{far}{j}{q}"], add_up)
            if j:
                links = {1: [ox + "+"], 2: [ox + "+", ox + "-"], 3: [ox + "-"]}[j]
                send(f"n{j}{q}", links, HALF, [f"a{j}{q}"], rows_of(p2send, r, HALF), rows_of(p2recv, r, HALF), dev(**{"d" + ox: j}), "SN")

                def gather_up(j=j, b=b, r=r):
                    imf[pl.ds(b, HALF), :] += decode(p2recv[pl.ds(r, HALF), :])

                g.op(f"o{j}{q}", 0.07, ["a0" + q, f"n{j}{q}"], gather_up)

    def image_end():
        for o, b in ((0, 0), (HALF, 128)):
            out_ref[pl.ds(o, HALF), :] = restore(x_ref[pl.ds(o, HALF), :], scale_ref[0] * imf[pl.ds(b, HALF), :])

    g.op("gx", 0.4, [f"o{j}{q}" for j in (1, 2, 3) for q in "ab"], image_end)
    sizes = {"SY": zsend, "SC": rows_of(xg, 0, 512), "SX": rows_of(xg, 0, 960), "SL": rows_of(lrecv, 0, 14), "SK": crecv, "SZ": zsend,
             "SI": isend, "SN": p2send, "R4": rows_of(xg, 0, 64), "RT": rows_of(xg, 0, 256), "RLc": lrecv.at[0],
             "RLz": rows_of(lrecv, 0, 7), "RLx": rows_of(lrecv, 0, 3), "RLy": rows_of(lrecv, 0, 3)}
    for n, t in g.tasks.items():
        if t["msg"] and t["come"] not in sizes:
            sizes[t["come"]] = rows_of(xg, 0, 64)
    g.emit(ssem, rsem, sizes)


def finish(grads_ref, loss_ref, gx_ref, gy_ref):
    gx_ref[...] = grads_ref[pl.ds(0, ROWS), :]
    gy_ref[...] = grads_ref[pl.ds(ROWS, ROWS), :]
    loss_ref[0] = grads_ref[2 * ROWS, 0]


SENT = 8
COME = 123


def local(picture_embeddings, caption_embeddings, sharpness_factor, pairing_shift):
    vmem = pl.BlockSpec(memory_space=pltpu.VMEM)
    smem = pl.BlockSpec(memory_space=pltpu.SMEM)
    hbm = pl.BlockSpec(memory_space=pltpu.HBM)
    grads = pl.pallas_call(
        kernel,
        out_shape=jax.ShapeDtypeStruct((2 * ROWS + 8, D), F32),
        in_specs=[hbm, hbm, hbm, hbm],
        out_specs=vmem,
        scratch_shapes=[
            pltpu.VMEM((1024, D), BF16),
            pltpu.VMEM((1024, D), BF16),
            pltpu.VMEM((1024, 1024), BF16),
            pltpu.VMEM((768, D), F32),
            pltpu.VMEM((768, D), BF16),
            pltpu.VMEM((768, D), BF16),
            pltpu.VMEM((192, D), BF16),
            pltpu.VMEM((192, D), BF16),
            pltpu.VMEM((1024, D), F32),
            pltpu.VMEM((512, D), F32),
            pltpu.VMEM((448, D), BF16),
            pltpu.VMEM((448, D), BF16),
            pltpu.VMEM((8, 128), F32),
            pltpu.VMEM((8, 128), F32),
            pltpu.VMEM((18, 8, 128), F32),
            pltpu.VMEM((ROWS, D), BF16),
            pltpu.VMEM((ROWS, D), BF16),
            pltpu.SMEM((1,), F32),
            pltpu.SMEM((1,), F32),
            pltpu.SemaphoreType.DMA((4,)),
            pltpu.SemaphoreType.DMA((SENT,)),
            pltpu.SemaphoreType.DMA((COME,)),
        ],
        compiler_params=pltpu.CompilerParams(collective_id=0, has_side_effects=True, vmem_limit_bytes=40 * 2**20),
    )(picture_embeddings, caption_embeddings, sharpness_factor, pairing_shift)
    return pl.pallas_call(
        finish,
        out_shape=(
            jax.ShapeDtypeStruct((1,), F32),
            jax.ShapeDtypeStruct((ROWS, D), F32),
            jax.ShapeDtypeStruct((ROWS, D), F32),
        ),
        in_specs=[vmem],
        out_specs=(smem, vmem, vmem),
        compiler_params=pltpu.CompilerParams(vmem_limit_bytes=4 * 2**20),
    )(grads)


def solution(mesh):
    in_specs = (P(("img", "txt"), None), P(("txt", "img"), None), P(), P())
    out_specs = (P(), P(("img", "txt"), None), P(("txt", "img"), None))
    return jax.shard_map(local, mesh=mesh, in_specs=in_specs, out_specs=out_specs, check_vma=False)
```

```python
import jax
import jax.numpy as jnp
from jax import lax
from jax.experimental import pallas as pl
from jax.experimental.pallas import tpu as pltpu
from jax.sharding import PartitionSpec as P

MESH = pl.DeviceIdType.MESH
F32 = jnp.float32
BF16 = jnp.bfloat16
ROWS = 64
HALF = 32
PIECE = 16
D = 1152
LOG2E = 1.4426950408889634
POS = {0: 0, 1: 1, 7: 2, 2: 3, 6: 4, 3: 5, 5: 6, 4: 7}
CHUNK = {0: 0, 1: 1, 3: 2, 2: 3}
RATE = {"core": 300.0}
LINK_RATE = 20.6
LATENCY = {"core": 1.0, 1: 2.2, 2: 3.0}
BACKLOG = 1.6
ISSUE = 0.03
WAIT = 0.015


class Schedule:
    def __init__(self):
        self.tasks = {}

    def op(self, name, cost, deps, fn):
        self.tasks[name] = dict(name=name, msg=False, cost=cost, deps=list(deps), fn=fn)

    def msg(self, name, links, rows, lat, deps, make, sent, come):
        took = max([rows / RATE.get(x, LINK_RATE) for x in links], default=0.0)
        self.tasks[name] = dict(name=name, msg=True, links=links, took=took, lat=lat, deps=list(deps), fn=make, sent=sent, come=come)

    def levels(self):
        users = {n: [] for n in self.tasks}
        for n, t in self.tasks.items():
            for d in t["deps"]:
                users[d].append(n)
        level = {}

        def visit(n):
            if n not in level:
                t = self.tasks[n]
                own = ISSUE + t["lat"] + t["took"] if t["msg"] else t["cost"]
                level[n] = own + max([visit(u) for u in users[n]], default=0.0)
            return level[n]

        for n in self.tasks:
            visit(n)
        return level

    def order(self):
        level = self.levels()
        now, arrived, free, out, waited = 0.0, {}, {}, [], set()
        left = list(self.tasks)
        self.times = {}
        while left:
            ready, later = [], []
            for n in left:
                t = self.tasks[n]
                if any(d not in arrived for d in t["deps"]):
                    continue
                at = max([arrived[d] for d in t["deps"]] + [free.get(x, 0.0) - BACKLOG for x in t.get("links", ())], default=0.0)
                if at <= now + 1e-9:
                    ready.append(n)
                else:
                    later.append(at)
            if not ready:
                now = min(later)
                continue
            n = max(ready, key=lambda n: (self.tasks[n]["msg"], level[n]))
            left.remove(n)
            out.append(n)
            t = self.tasks[n]
            for d in t["deps"]:
                if self.tasks[d]["msg"] and d not in waited:
                    waited.add(d)
                    now += WAIT
            if t["msg"]:
                now += ISSUE
                end = max([now] + [free.get(x, 0.0) for x in t["links"]]) + t["took"]
                for x in t["links"]:
                    free[x] = end
                arrived[n] = end + t["lat"]
            else:
                now += t["cost"]
                arrived[n] = now
            self.times[n] = now
        return out

    def emit(self, ssem, rsem, sizes):
        number = {True: {}, False: {}}
        members = {}
        for n, t in self.tasks.items():
            if t["msg"]:
                number[True].setdefault(t["sent"], len(number[True]))
                number[False].setdefault(t["come"], len(number[False]))
                members.setdefault(t["come"], []).append(n)
        assert len(number[True]) <= SENT and len(number[False]) <= COME, "semaphores"
        copies, received = {}, set()

        def wait_group(sem, ref):
            pltpu.make_async_copy(ref, ref, sem).wait()

        def receive(come):
            if come in received:
                return
            received.add(come)
            assert all(m in copies for m in members[come]), "group"
            if len(members[come]) == 1:
                copies[members[come][0]].wait_recv()
            else:
                wait_group(rsem.at[number[False][come]], sizes[come])

        for n in self.order():
            t = self.tasks[n]
            for d in t["deps"]:
                if self.tasks[d]["msg"]:
                    receive(self.tasks[d]["come"])
            if t["msg"]:
                copies[n] = t["fn"](ssem.at[number[True][t["sent"]]], rsem.at[number[False][t["come"]]])
                copies[n].start()
            else:
                t["fn"]()
        for come in members:
            receive(come)
        for sent, i in number[True].items():
            wait_group(ssem.at[i], sizes[sent])


def encode(v):
    return (v * jnp.abs(v)).astype(BF16)


def decode(u):
    u = u.astype(F32)
    return u * lax.rsqrt(jnp.maximum(jnp.abs(u), 1e-37))


def log1p(p):
    small = p * (1.0 - p * (0.5 - p * (1.0 / 3.0 - p * 0.25)))
    return jnp.where(p < 0.01, small, jnp.log(1.0 + p))


def restore(raw, grads):
    values = raw.astype(F32)
    inverse = lax.rsqrt(jnp.sum(values * values, axis=1, keepdims=True) + 1e-06)
    inner = jnp.sum(values * grads, axis=1, keepdims=True)
    return inverse * grads - inverse * inverse * inverse * values * inner


def kernel(x_hbm, y_hbm, scale_hbm, shift_hbm, out_ref,
           xg, yg, w, imf, isend, irecv, p2send, p2recv, tf, crecv, zsend, zrecv,
           lacc, lsum, lrecv, x_ref, y_ref, scale_ref, shift_ref, csem, ssem, rsem):
    img, txt = lax.axis_index("img"), lax.axis_index("txt")
    Y, C = img // 2, img % 2
    X, Z = txt // 8, txt % 8

    def dev(dx=0, dy=0, dz=0, dc=0):
        return (((Y + dy) % 4) * 2 + (C + dc) % 2, ((X + dx) % 4) * 8 + (Z + dz) % 8)

    inputs = [pltpu.make_async_copy(a, b, csem.at[i]) for i, (a, b) in enumerate(
        ((y_hbm, y_ref), (x_hbm, x_ref), (scale_hbm, scale_ref), (shift_hbm, shift_ref)))]
    for c in inputs:
        c.start()
    barrier = pltpu.get_barrier_semaphore()
    peers = ([dev(dz=1), dev(dz=-1)] + [dev(dx=i) for i in (1, 2, 3)] + [dev(dy=i) for i in (1, 2, 3)]
             + [dev(dc=1)])
    for p in peers:
        pl.semaphore_signal(barrier, inc=1, device_id=p, device_id_type=MESH)

    def unit(ref):
        values = ref[...].astype(F32)
        inverse = lax.rsqrt(jnp.sum(values * values, axis=1, keepdims=True) + 1e-06)
        return (values * inverse).astype(BF16)

    def A(k, j):
        return CHUNK[k] * 256 + j * HALF

    def B(k, j):
        return CHUNK[k] * 256 + 128 + j * HALF

    def yrow(s, rc):
        return POS[s] * 128 + rc * ROWS

    g = Schedule()

    def send(name, links, rows, deps, src, dst, to, sent, come=None, lat=None):
        if lat is None:
            lat = LATENCY["core"] if links == ["core"] else LATENCY[max(1, len(links))]
        g.msg(name, links, rows, lat, deps, lambda ss, rs: pltpu.make_async_remote_copy(
            src_ref=src, dst_ref=dst, send_sem=ss, recv_sem=rs, device_id=to, device_id_type=MESH), sent, come or name)

    def own_text():
        inputs[0].wait()
        yg[pl.ds(yrow(0, 0), ROWS)] = unit(y_ref)
        pl.semaphore_wait(barrier, len(peers))

    def own_image():
        inputs[1].wait()
        xn = unit(x_ref)
        xg[pl.ds(A(0, 0), HALF)] = xn[:HALF]
        xg[pl.ds(B(0, 0), HALF)] = xn[HALF:]
        lacc[...] = jnp.zeros_like(lacc)
        for c in inputs[2:]:
            c.wait()

    g.op("ny", 0.3, [], own_text)
    g.op("nx", 0.3, ["ny"], own_image)

    def rows_of(ref, start, n):
        return ref.at[pl.ds(start, n)]

    for t in (1, 2, 3, 4):
        for h in range(ROWS // PIECE):
            o = h * PIECE
            if t < 4 or o < HALF:
                send(f"u{t}{h}", ["z+"], PIECE, [f"u{t - 1}{h}"] if t > 1 else ["ny"],
                     rows_of(yg, yrow((9 - t) % 8, 0) + o, PIECE), rows_of(yg, yrow(8 - t, 0) + o, PIECE), dev(dz=1), "SY", "R4" if t == 4 else None)
            if t < 4 or o >= HALF:
                send(f"d{t}{h}", ["z-"], PIECE, [f"d{t - 1}{h}"] if t > 1 else ["ny"],
                     rows_of(yg, yrow(t - 1, 0) + o, PIECE), rows_of(yg, yrow(t, 0) + o, PIECE), dev(dz=-1), "SY", "R4" if t == 4 else None)
    pieces = range(ROWS // PIECE)
    yhave = {0: ["ny"], 4: [f"u4{h}" for h in pieces if h * PIECE < HALF] + [f"d4{h}" for h in pieces if h * PIECE >= HALF]}
    for t in (1, 2, 3):
        yhave[8 - t] = [f"u{t}{h}" for h in pieces]
        yhave[t] = [f"d{t}{h}" for h in pieces]
    for s in range(8):
        send(f"c{s}", ["core"], ROWS, yhave[s], rows_of(yg, yrow(s, 0), ROWS), rows_of(yg, yrow(s, 1), ROWS), dev(dc=1), "SC")

    def both(name, d, rows, da, db, a, a2, b, b2, n):
        links = {1: ["{}+"], 3: ["{}-"], 2: ["{}+", "{}-"]}[d % 4]
        first = name[0] == "f"
        come = "RT" if name[0] == "t" else "R" + name
        ax, bx = ("x", "y") if first else ("y", "x")
        send(name + "a", [x.format(ax) for x in links], rows, da, rows_of(xg, a, n), rows_of(xg, a2, n), dev(**{"d" + ax: d}), "SX", come)
        send(name + "b", [x.format(bx) for x in links], rows, db, rows_of(xg, b, n), rows_of(xg, b2, n), dev(**{"d" + bx: d}), "SX", come)

    for j, d in ((3, 1), (1, -1), (2, 2)):
        both(f"f{j}", d, HALF, ["nx"], ["nx"], A(0, 0), A(0, j), B(0, 0), B(0, j), HALF)
    for j in range(4):
        for k, d in ((3, 1), (1, -1)):
            da = db = [f"f{j}a", f"f{j}b"] if j else ["nx"]
            both(f"s{k}{j}", d, HALF, da, db, A(0, j), A(k, j), B(0, j), B(k, j), HALF)
            o = 16 if k == 3 else 0
            both(f"t{k}{j}", d, 16, [f"s{k}{j}a", f"s{k}{j}b"], [f"s{k}{j}a", f"s{k}{j}b"], A(k, j) + o, A(2, j) + o, B(k, j) + o, B(2, j) + o, 16)
    xhave = {0: [f"f{j}{q}" for j in (1, 2, 3) for q in "ab"], 2: [f"t{k}{j}{q}" for k in (1, 3) for j in range(4) for q in "ab"]}
    for k in (1, 3):
        xhave[k] = [f"s{k}{j}{q}" for j in range(4) for q in "ab"]

    def tile(r0, nr, c0, nc):
        def run():
            dots = lax.dot_general(xg[pl.ds(r0, nr), :], yg[pl.ds(c0, nc), :], (((1,), (1,)), ((), ())),
                                   preferred_element_type=F32)
            e = jnp.exp2(dots * (scale_ref[0] * LOG2E) + shift_ref[0] * LOG2E)
            d = 1.0 + e
            r = pl.reciprocal(d, approx=True)
            r = r * (2.0 - d * r)
            w[pl.ds(r0, nr), pl.ds(c0, nc)] = (e * r).astype(BF16)
            m = nr // 8
            n = m // 3
            e, d = e.reshape(m, 8, nc), d.reshape(m, 8, nc)
            p = e[:n] * d[n : 2 * n] + e[n : 2 * n]
            p = p * d[2 * n : 3 * n] + e[2 * n : 3 * n]
            total = jnp.sum(log1p(p), axis=0)
            if m - 3 * n == 2:
                total += log1p(e[m - 2] * d[m - 1] + e[m - 1])
            elif m - 3 * n == 1:
                total += log1p(e[m - 1])
            for c in range(0, nc, 128):
                lacc[...] += total[:, c : c + 128]

        return run

    groups = {"a": (0, 384, (0, 1, 7)), "b": (384, 256, (2, 6)), "c": (640, 256, (3, 5)), "d": (896, 128, (4,))}
    tiles = []

    def add_tile(chunks, cols, cost):
        r0 = min(CHUNK[k] for k in chunks) * 256
        c0 = min(groups[c][0] for c in cols)
        nc = sum(groups[c][1] for c in cols)
        deps = sum([xhave[k] for k in chunks], [])
        for c in cols:
            for s in groups[c][2]:
                deps = deps + yhave[s] + [f"c{s}"]
        tiles.append("w" + "".join(map(str, chunks)) + cols)
        g.op(tiles[-1], cost, deps, tile(r0, 256 * len(chunks), c0, nc))

    add_tile((0,), "a", 0.58)
    add_tile((0,), "b", 0.44)
    add_tile((0,), "c", 0.44)
    add_tile((1, 3), "a", 1.0)
    add_tile((1, 3), "b", 0.72)
    add_tile((1, 3), "c", 0.72)
    add_tile((2,), "abcd", 1.3)
    add_tile((0, 1, 3), "d", 0.6)

    def positives():
        @pl.when(Y == Z // 2)
        def _():
            rc = (Z + C) % 2
            blocks = []
            for xx in range(4):
                for h in (0, 1):
                    k, j = (X - Y + 4) % 4, (xx - X + 4) % 4
                    if h == 1:
                        k, j = j, k
                    row = pl.multiple_of(jnp.where(k < 2, k, 5 - k) * 256 + h * 128 + j * HALF, HALF)
                    s = (4 * C + xx - Z + 8) % 8
                    pos = jnp.where(s == 0, 0, jnp.where(s == 4, 7, jnp.where(s < 4, 2 * s - 1, 2 * (8 - s))))
                    col = pl.multiple_of(pos * 128, 128)
                    yr = pl.multiple_of(pos * 128 + rc * ROWS + h * HALF, HALF)
                    xv = xg[pl.ds(row, HALF), :].astype(F32)
                    yv = yg[pl.ds(yr, HALF), :].astype(F32)
                    z = scale_ref[0] * jnp.sum(xv * yv, axis=1, keepdims=True) + shift_ref[0]
                    blocks.append((row, col, h, z, w[pl.ds(row, HALF), pl.ds(col, 128)]))
            less = jnp.zeros((8, 128), F32)
            lane = lax.broadcasted_iota(jnp.int32, (HALF, 128), 1)
            sub = lax.broadcasted_iota(jnp.int32, (HALF, 128), 0)
            for row, col, h, z, old in blocks:
                e = jnp.exp(z)
                wd = (e / (1.0 + e) - 1.0).astype(BF16)
                hit = lane == sub + rc * ROWS + h * HALF
                w[pl.ds(row, HALF), pl.ds(col, 128)] = jnp.where(hit, wd.astype(F32), old.astype(F32)).astype(BF16)
                less += jnp.sum(jnp.where(hit, z, 0.0).reshape(4, 8, 128), axis=0)
            lacc[...] -= less

    g.op("pos", 0.4, tiles, positives)
    fixed = ["pos"]

    def loss_axis(axis, before):
        n, me, base, kw, lat = {"c": (2, C, 0, "dc", 0.8), "z": (8, Z, 2, "dz", 4.0), "x": (4, X, 10, "dx", 2.6),
                                "y": (4, Y, 14, "dy", 2.6)}[axis]

        def run():
            if before is None:
                v = jnp.full((8, 128), jnp.sum(lacc[...]), F32)
            else:
                b, m = before
                v = lrecv[b]
                for o in range(1, m):
                    v = v + lrecv[b + o]
            lrecv[base + me] = v

        prev = {"c": "", "z": "c", "x": "z", "y": "x"}[axis]
        hops = ("zu1", "zu2", "zu3", "zu4", "zd1", "zd2", "zd3")
        deps = fixed if axis == "c" else ["l" + prev] + ([f"l{q}" for q in hops] if prev == "z" else [f"l{prev}{o}" for o in range(1, {"c": 2, "x": 4}[prev])])
        g.op("l" + axis, 0.1, deps, run)
        if axis == "z":
            for q, sign, far in (("u", 1, 4), ("d", -1, 3)):
                for t in range(1, far + 1):
                    at = base + (Z - sign * (t - 1) + 8) % 8
                    send(f"lz{q}{t}", [], 0, [f"lz{q}{t - 1}" if t > 1 else "lz"], lrecv.at[at], lrecv.at[at], dev(dz=sign), "SL")
            return
        for o in range(1, n):
            send(f"l{axis}{o}", [], 0, ["l" + axis], lrecv.at[base + me], lrecv.at[base + me], dev(**{kw: o}), "SL", "RL" + axis, lat)

    loss_axis("c", None)
    loss_axis("z", (0, 2))
    loss_axis("x", (2, 8))
    loss_axis("y", (10, 4))

    def loss_end():
        v = lrecv[14]
        for o in range(1, 4):
            v = v + lrecv[14 + o]
        lsum[...] = v
        out_ref[pl.ds(2 * ROWS, 8), pl.ds(0, 128)] = lsum[...] * (1.0 / 16384.0)

    g.op("loss", 0.1, ["ly"] + [f"ly{o}" for o in (1, 2, 3)], loss_end)

    def text(c0, nc):
        def run():
            tf[pl.ds(c0, nc), :] = lax.dot_general(w[:, pl.ds(c0, nc)], xg[...], (((0,), (0,)), ((), ())),
                                                   preferred_element_type=F32)

        return run

    for n, c0, nc, slots in (("4", 896, 128, (4,)), ("35", 640, 256, (3, 5)), ("26", 384, 256, (2, 6)),
                             ("17", 128, 256, (1, 7)), ("0", 0, 128, (0,))):
        g.op("x" + n, 0.06 + 0.52 * nc / 256, fixed, text(c0, nc))
        for s in slots:
            send(f"x{n}c{s}", ["core"], 2 * ROWS, ["x" + n], rows_of(tf, yrow(s, 1), ROWS), rows_of(crecv, s * ROWS, ROWS), dev(dc=1), "SK")

            def add(s=s):
                tf[pl.ds(yrow(s, 0), ROWS), :] += crecv[pl.ds(s * ROWS, ROWS), :]

            g.op(f"k{s}", 0.07, ["x" + n, f"x{n}c{s}"], add)

    slot = 0
    for sign, q in ((1, "p"), (-1, "m")):
        for h in pieces:
            first = 4 if (sign > 0) == (h * PIECE < HALF) else 3
            for t in range(first, 0, -1):
                s = t if sign > 0 else 8 - t
                deps = [f"k{s}"] + ([f"z{q}{t + 1}{h}"] if t < first else [])
                r = slot * PIECE

                def hop(s=s, h=h, r=r, more=t < first):
                    v = tf[pl.ds(yrow(s, 0) + h * PIECE, PIECE), :]
                    if more:
                        v = v + decode(zrecv[pl.ds(r - PIECE, PIECE), :])
                    zsend[pl.ds(r, PIECE), :] = encode(v)

                g.op(f"h{q}{t}{h}", 0.04 + 0.0014 * PIECE, deps, hop)
                send(f"z{q}{t}{h}", ["z+" if sign > 0 else "z-"], PIECE, [f"h{q}{t}{h}"], rows_of(zsend, r, PIECE), rows_of(zrecv, r, PIECE), dev(dz=sign), "SZ")
                slot += 1

            def last(h=h, r=r):
                tf[pl.ds(yrow(0, 0) + h * PIECE, PIECE), :] += decode(zrecv[pl.ds(r, PIECE), :])

            g.op(f"e{q}{h}", 0.06, ["k0", f"z{q}1{h}"], last)

    def text_end():
        out_ref[pl.ds(ROWS, ROWS), :] = restore(y_ref[...], scale_ref[0] * tf[pl.ds(yrow(0, 0), ROWS), :])

    g.op("gy", 0.3, [f"e{q}{h}" for q in "pm" for h in pieces], text_end)

    def image(k):
        def run():
            part = jnp.dot(w[pl.ds(CHUNK[k] * 256, 256), :], yg[...], preferred_element_type=F32)
            if k == 2:
                isend[pl.ds(0, 256), :] = encode(part)
                return
            imf[pl.ds(CHUNK[k] * 256, 256), :] = part
            if k:
                for b in (0, 128):
                    o = CHUNK[k] * 256 + b + (64 if k == 1 else 0)
                    isend[pl.ds(o, 64), :] = encode(imf[pl.ds(o, 64), :])

        return run

    for k in (0, 1, 2, 3):
        g.op(f"i{k}", 0.7, ["pos"], image(k))
    for q, b, ax in (("a", 0, "y"), ("b", 128, "x")):
        def part(name, start, deps, d, b=b, ax=ax, q=q):
            send(name + q, [ax + ("+" if d > 0 else "-")], HALF, deps, rows_of(isend, start + b, HALF), rows_of(irecv, start + b, HALF),
                 dev(**{"d" + ax: d}), "SI")

        ox = "x" if q == "a" else "y"
        for j in (1, 2, 0, 3):
            near, far, d = (1, 3, 1) if j in (0, 1) else (3, 1, -1)
            o2, on, of = j * HALF, CHUNK[near] * 256 + j * HALF, CHUNK[far] * 256 + j * HALF
            part(f"m2{j}", o2, ["i2"], d)
            part(f"m{far}{j}", of, [f"i{far}"], -d)

            def join(on=on, o2=o2, b=b):
                v = imf[pl.ds(on + b, HALF), :] + decode(irecv[pl.ds(o2 + b, HALF), :])
                isend[pl.ds(on + b, HALF), :] = encode(v)

            g.op(f"j{j}{q}", 0.1, [f"i{near}", f"m2{j}{q}"], join)
            part(f"m{near}{j}", on, [f"j{j}{q}"], d)
            r = (2 * (j - 1) + b // 128) * HALF

            def add_up(j=j, b=b, on=on, of=of, r=r):
                v = imf[pl.ds(b + j * HALF, HALF), :] + decode(irecv[pl.ds(on + b, HALF), :]) + decode(irecv[pl.ds(of + b, HALF), :])
                if j:
                    p2send[pl.ds(r, HALF), :] = encode(v)
                else:
                    imf[pl.ds(b, HALF), :] = v

            g.op(f"a{j}{q}", 0.12, ["i0", f"m{near}{j}{q}", f"m{far}{j}{q}"], add_up)
            if j:
                links = {1: [ox + "+"], 2: [ox + "+", ox + "-"], 3: [ox + "-"]}[j]
                send(f"n{j}{q}", links, HALF, [f"a{j}{q}"], rows_of(p2send, r, HALF), rows_of(p2recv, r, HALF), dev(**{"d" + ox: j}), "SN")

                def gather_up(j=j, b=b, r=r):
                    imf[pl.ds(b, HALF), :] += decode(p2recv[pl.ds(r, HALF), :])

                g.op(f"o{j}{q}", 0.07, ["a0" + q, f"n{j}{q}"], gather_up)

    def image_end():
        for o, b in ((0, 0), (HALF, 128)):
            out_ref[pl.ds(o, HALF), :] = restore(x_ref[pl.ds(o, HALF), :], scale_ref[0] * imf[pl.ds(b, HALF), :])

    g.op("gx", 0.4, [f"o{j}{q}" for j in (1, 2, 3) for q in "ab"], image_end)
    sizes = {"SY": zsend, "SC": rows_of(xg, 0, 512), "SX": rows_of(xg, 0, 960), "SL": rows_of(lrecv, 0, 14), "SK": crecv, "SZ": zsend,
             "SI": isend, "SN": p2send, "R4": rows_of(xg, 0, 64), "RT": rows_of(xg, 0, 256), "RLc": lrecv.at[0],
             "RLz": rows_of(lrecv, 0, 7), "RLx": rows_of(lrecv, 0, 3), "RLy": rows_of(lrecv, 0, 3)}
    for n, t in g.tasks.items():
        if t["msg"] and t["come"] not in sizes:
            sizes[t["come"]] = rows_of(xg, 0, 64)
    g.emit(ssem, rsem, sizes)


def finish(grads_ref, loss_ref, gx_ref, gy_ref):
    gx_ref[...] = grads_ref[pl.ds(0, ROWS), :]
    gy_ref[...] = grads_ref[pl.ds(ROWS, ROWS), :]
    loss_ref[0] = grads_ref[2 * ROWS, 0]


SENT = 8
COME = 123


def local(picture_embeddings, caption_embeddings, sharpness_factor, pairing_shift):
    vmem = pl.BlockSpec(memory_space=pltpu.VMEM)
    smem = pl.BlockSpec(memory_space=pltpu.SMEM)
    hbm = pl.BlockSpec(memory_space=pltpu.HBM)
    grads = pl.pallas_call(
        kernel,
        out_shape=jax.ShapeDtypeStruct((2 * ROWS + 8, D), F32),
        in_specs=[hbm, hbm, hbm, hbm],
        out_specs=vmem,
        scratch_shapes=[
            pltpu.VMEM((1024, D), BF16),
            pltpu.VMEM((1024, D), BF16),
            pltpu.VMEM((1024, 1024), BF16),
            pltpu.VMEM((768, D), F32),
            pltpu.VMEM((768, D), BF16),
            pltpu.VMEM((768, D), BF16),
            pltpu.VMEM((192, D), BF16),
            pltpu.VMEM((192, D), BF16),
            pltpu.VMEM((1024, D), F32),
            pltpu.VMEM((512, D), F32),
            pltpu.VMEM((448, D), BF16),
            pltpu.VMEM((448, D), BF16),
            pltpu.VMEM((8, 128), F32),
            pltpu.VMEM((8, 128), F32),
            pltpu.VMEM((18, 8, 128), F32),
            pltpu.VMEM((ROWS, D), BF16),
            pltpu.VMEM((ROWS, D), BF16),
            pltpu.SMEM((1,), F32),
            pltpu.SMEM((1,), F32),
            pltpu.SemaphoreType.DMA((4,)),
            pltpu.SemaphoreType.DMA((SENT,)),
            pltpu.SemaphoreType.DMA((COME,)),
        ],
        compiler_params=pltpu.CompilerParams(collective_id=0, has_side_effects=True, vmem_limit_bytes=40 * 2**20),
    )(picture_embeddings, caption_embeddings, sharpness_factor, pairing_shift)
    return pl.pallas_call(
        finish,
        out_shape=(
            jax.ShapeDtypeStruct((1,), F32),
            jax.ShapeDtypeStruct((ROWS, D), F32),
            jax.ShapeDtypeStruct((ROWS, D), F32),
        ),
        in_specs=[vmem],
        out_specs=(smem, vmem, vmem),
        compiler_params=pltpu.CompilerParams(vmem_limit_bytes=4 * 2**20),
    )(grads)


def solution(mesh):
    in_specs = (P(("img", "txt"), None), P(("txt", "img"), None), P(), P())
    out_specs = (P(), P(("img", "txt"), None), P(("txt", "img"), None))
    return jax.shard_map(local, mesh=mesh, in_specs=in_specs, out_specs=out_specs, check_vma=False)
```

```python
import jax
import jax.numpy as jnp
from jax import lax
from jax.experimental import pallas as pl
from jax.experimental.pallas import tpu as pltpu
from jax.sharding import PartitionSpec as P

MESH = pl.DeviceIdType.MESH
F32 = jnp.float32
BF16 = jnp.bfloat16
ROWS = 64
HALF = 32
PIECE = 16
D = 1152
LOG2E = 1.4426950408889634
POS = {0: 0, 1: 1, 7: 2, 2: 3, 6: 4, 3: 5, 5: 6, 4: 7}
CHUNK = {0: 0, 1: 1, 3: 2, 2: 3}
RATE = {"core": 300.0}
LINK_RATE = 20.6
LATENCY = {"core": 1.0, 1: 2.2, 2: 3.0}
BACKLOG = 1.6
ISSUE = 0.03
WAIT = 0.015


class Schedule:
    def __init__(self):
        self.tasks = {}

    def op(self, name, cost, deps, fn):
        self.tasks[name] = dict(name=name, msg=False, cost=cost, deps=list(deps), fn=fn)

    def msg(self, name, links, rows, lat, deps, make, sent, come):
        took = max([rows / RATE.get(x, LINK_RATE) for x in links], default=0.0)
        self.tasks[name] = dict(name=name, msg=True, links=links, took=took, lat=lat, deps=list(deps), fn=make, sent=sent, come=come)

    def levels(self):
        users = {n: [] for n in self.tasks}
        for n, t in self.tasks.items():
            for d in t["deps"]:
                users[d].append(n)
        level = {}

        def visit(n):
            if n not in level:
                t = self.tasks[n]
                own = ISSUE + t["lat"] + t["took"] if t["msg"] else t["cost"]
                level[n] = own + max([visit(u) for u in users[n]], default=0.0)
            return level[n]

        for n in self.tasks:
            visit(n)
        return level

    def order(self):
        level = self.levels()
        now, arrived, free, out, waited = 0.0, {}, {}, [], set()
        left = list(self.tasks)
        self.times = {}
        while left:
            ready, later = [], []
            for n in left:
                t = self.tasks[n]
                if any(d not in arrived for d in t["deps"]):
                    continue
                at = max([arrived[d] for d in t["deps"]] + [free.get(x, 0.0) - BACKLOG for x in t.get("links", ())], default=0.0)
                if at <= now + 1e-9:
                    ready.append(n)
                else:
                    later.append(at)
            if not ready:
                now = min(later)
                continue
            n = max(ready, key=lambda n: (self.tasks[n]["msg"], n[0] == "l", level[n]))
            left.remove(n)
            out.append(n)
            t = self.tasks[n]
            for d in t["deps"]:
                if self.tasks[d]["msg"] and d not in waited:
                    waited.add(d)
                    now += WAIT
            if t["msg"]:
                now += ISSUE
                end = max([now] + [free.get(x, 0.0) for x in t["links"]]) + t["took"]
                for x in t["links"]:
                    free[x] = end
                arrived[n] = end + t["lat"]
            else:
                now += t["cost"]
                arrived[n] = now
            self.times[n] = now
        return out

    def emit(self, ssem, rsem, sizes):
        number = {True: {}, False: {}}
        members = {}
        for n, t in self.tasks.items():
            if t["msg"]:
                number[True].setdefault(t["sent"], len(number[True]))
                number[False].setdefault(t["come"], len(number[False]))
                members.setdefault(t["come"], []).append(n)
        assert len(number[True]) <= SENT and len(number[False]) <= COME, "semaphores"
        copies, received = {}, set()

        def wait_group(sem, ref):
            pltpu.make_async_copy(ref, ref, sem).wait()

        def receive(come):
            if come in received:
                return
            received.add(come)
            assert all(m in copies for m in members[come]), "group"
            if len(members[come]) == 1:
                copies[members[come][0]].wait_recv()
            else:
                wait_group(rsem.at[number[False][come]], sizes[come])

        for n in self.order():
            t = self.tasks[n]
            for d in t["deps"]:
                if self.tasks[d]["msg"]:
                    receive(self.tasks[d]["come"])
            if t["msg"]:
                copies[n] = t["fn"](ssem.at[number[True][t["sent"]]], rsem.at[number[False][t["come"]]])
                copies[n].start()
            else:
                t["fn"]()
        for come in members:
            receive(come)
        for sent, i in number[True].items():
            wait_group(ssem.at[i], sizes[sent])


def encode(v):
    return (v * jnp.abs(v)).astype(BF16)


def decode(u):
    u = u.astype(F32)
    return u * lax.rsqrt(jnp.maximum(jnp.abs(u), 1e-37))


def log1p(p):
    small = p * (1.0 - p * (0.5 - p * (1.0 / 3.0 - p * 0.25)))
    return jnp.where(p < 0.01, small, jnp.log(1.0 + p))


def restore(raw, grads):
    values = raw.astype(F32)
    inverse = lax.rsqrt(jnp.sum(values * values, axis=1, keepdims=True) + 1e-06)
    inner = jnp.sum(values * grads, axis=1, keepdims=True)
    return inverse * grads - inverse * inverse * inverse * values * inner


def kernel(x_hbm, y_hbm, scale_hbm, shift_hbm, out_ref,
           xg, yg, w, imf, isend, irecv, p2send, p2recv, tf, crecv, zsend, zrecv,
           lacc, lsum, lrecv, x_ref, y_ref, scale_ref, shift_ref, csem, ssem, rsem):
    img, txt = lax.axis_index("img"), lax.axis_index("txt")
    Y, C = img // 2, img % 2
    X, Z = txt // 8, txt % 8

    def dev(dx=0, dy=0, dz=0, dc=0):
        return (((Y + dy) % 4) * 2 + (C + dc) % 2, ((X + dx) % 4) * 8 + (Z + dz) % 8)

    inputs = [pltpu.make_async_copy(a, b, csem.at[i]) for i, (a, b) in enumerate(
        ((y_hbm, y_ref), (x_hbm, x_ref), (scale_hbm, scale_ref), (shift_hbm, shift_ref)))]
    for c in inputs:
        c.start()
    barrier = pltpu.get_barrier_semaphore()
    peers = ([dev(dz=1), dev(dz=-1)] + [dev(dx=i) for i in (1, 2, 3)] + [dev(dy=i) for i in (1, 2, 3)]
             + [dev(dc=1)])
    for p in peers:
        pl.semaphore_signal(barrier, inc=1, device_id=p, device_id_type=MESH)

    def unit(ref):
        values = ref[...].astype(F32)
        inverse = lax.rsqrt(jnp.sum(values * values, axis=1, keepdims=True) + 1e-06)
        return (values * inverse).astype(BF16)

    def A(k, j):
        return CHUNK[k] * 256 + j * HALF

    def B(k, j):
        return CHUNK[k] * 256 + 128 + j * HALF

    def yrow(s, rc):
        return POS[s] * 128 + rc * ROWS

    g = Schedule()

    def send(name, links, rows, deps, src, dst, to, sent, come=None, lat=None):
        if lat is None:
            lat = LATENCY["core"] if links == ["core"] else LATENCY[max(1, len(links))]
        g.msg(name, links, rows, lat, deps, lambda ss, rs: pltpu.make_async_remote_copy(
            src_ref=src, dst_ref=dst, send_sem=ss, recv_sem=rs, device_id=to, device_id_type=MESH), sent, come or name)

    def own_text():
        inputs[0].wait()
        yg[pl.ds(yrow(0, 0), ROWS)] = unit(y_ref)
        pl.semaphore_wait(barrier, len(peers))

    def own_image():
        inputs[1].wait()
        xn = unit(x_ref)
        xg[pl.ds(A(0, 0), HALF)] = xn[:HALF]
        xg[pl.ds(B(0, 0), HALF)] = xn[HALF:]
        lacc[...] = jnp.zeros_like(lacc)
        for c in inputs[2:]:
            c.wait()

    g.op("ny", 0.3, [], own_text)
    g.op("nx", 0.3, ["ny"], own_image)

    def rows_of(ref, start, n):
        return ref.at[pl.ds(start, n)]

    for t in (1, 2, 3, 4):
        for h in range(ROWS // PIECE):
            o = h * PIECE
            if t < 4 or o < HALF:
                send(f"u{t}{h}", ["z+"], PIECE, [f"u{t - 1}{h}"] if t > 1 else ["ny"],
                     rows_of(yg, yrow((9 - t) % 8, 0) + o, PIECE), rows_of(yg, yrow(8 - t, 0) + o, PIECE), dev(dz=1), "SY", "R4" if t == 4 else None)
            if t < 4 or o >= HALF:
                send(f"d{t}{h}", ["z-"], PIECE, [f"d{t - 1}{h}"] if t > 1 else ["ny"],
                     rows_of(yg, yrow(t - 1, 0) + o, PIECE), rows_of(yg, yrow(t, 0) + o, PIECE), dev(dz=-1), "SY", "R4" if t == 4 else None)
    pieces = range(ROWS // PIECE)
    yhave = {0: ["ny"], 4: [f"u4{h}" for h in pieces if h * PIECE < HALF] + [f"d4{h}" for h in pieces if h * PIECE >= HALF]}
    for t in (1, 2, 3):
        yhave[8 - t] = [f"u{t}{h}" for h in pieces]
        yhave[t] = [f"d{t}{h}" for h in pieces]
    for s in range(8):
        send(f"c{s}", ["core"], ROWS, yhave[s], rows_of(yg, yrow(s, 0), ROWS), rows_of(yg, yrow(s, 1), ROWS), dev(dc=1), "SC")

    def both(name, d, rows, da, db, a, a2, b, b2, n):
        links = {1: ["{}+"], 3: ["{}-"], 2: ["{}+", "{}-"]}[d % 4]
        first = name[0] == "f"
        come = "RT" if name[0] == "t" else "R" + name
        ax, bx = ("x", "y") if first else ("y", "x")
        send(name + "a", [x.format(ax) for x in links], rows, da, rows_of(xg, a, n), rows_of(xg, a2, n), dev(**{"d" + ax: d}), "SX", come)
        send(name + "b", [x.format(bx) for x in links], rows, db, rows_of(xg, b, n), rows_of(xg, b2, n), dev(**{"d" + bx: d}), "SX", come)

    for j, d in ((3, 1), (1, -1), (2, 2)):
        both(f"f{j}", d, HALF, ["nx"], ["nx"], A(0, 0), A(0, j), B(0, 0), B(0, j), HALF)
    for j in range(4):
        for k, d in ((3, 1), (1, -1)):
            da = db = [f"f{j}a", f"f{j}b"] if j else ["nx"]
            both(f"s{k}{j}", d, HALF, da, db, A(0, j), A(k, j), B(0, j), B(k, j), HALF)
            o = 16 if k == 3 else 0
            both(f"t{k}{j}", d, 16, [f"s{k}{j}a", f"s{k}{j}b"], [f"s{k}{j}a", f"s{k}{j}b"], A(k, j) + o, A(2, j) + o, B(k, j) + o, B(2, j) + o, 16)
    xhave = {0: [f"f{j}{q}" for j in (1, 2, 3) for q in "ab"], 2: [f"t{k}{j}{q}" for k in (1, 3) for j in range(4) for q in "ab"]}
    for k in (1, 3):
        xhave[k] = [f"s{k}{j}{q}" for j in range(4) for q in "ab"]

    def tile(r0, nr, c0, nc):
        def run():
            dots = lax.dot_general(xg[pl.ds(r0, nr), :], yg[pl.ds(c0, nc), :], (((1,), (1,)), ((), ())),
                                   preferred_element_type=F32)
            e = jnp.exp2(dots * (scale_ref[0] * LOG2E) + shift_ref[0] * LOG2E)
            d = 1.0 + e
            r = pl.reciprocal(d, approx=True)
            r = r * (2.0 - d * r)
            w[pl.ds(r0, nr), pl.ds(c0, nc)] = (e * r).astype(BF16)
            m = nr // 8
            n = m // 3
            e, d = e.reshape(m, 8, nc), d.reshape(m, 8, nc)
            p = e[:n] * d[n : 2 * n] + e[n : 2 * n]
            p = p * d[2 * n : 3 * n] + e[2 * n : 3 * n]
            total = jnp.sum(log1p(p), axis=0)
            if m - 3 * n == 2:
                total += log1p(e[m - 2] * d[m - 1] + e[m - 1])
            elif m - 3 * n == 1:
                total += log1p(e[m - 1])
            for c in range(0, nc, 128):
                lacc[...] += total[:, c : c + 128]

        return run

    groups = {"a": (0, 384, (0, 1, 7)), "b": (384, 256, (2, 6)), "c": (640, 256, (3, 5)), "d": (896, 128, (4,))}
    tiles = []

    def add_tile(chunks, cols, cost):
        r0 = min(CHUNK[k] for k in chunks) * 256
        c0 = min(groups[c][0] for c in cols)
        nc = sum(groups[c][1] for c in cols)
        deps = sum([xhave[k] for k in chunks], [])
        for c in cols:
            for s in groups[c][2]:
                deps = deps + yhave[s] + [f"c{s}"]
        tiles.append("w" + "".join(map(str, chunks)) + cols)
        g.op(tiles[-1], cost, deps, tile(r0, 256 * len(chunks), c0, nc))

    add_tile((0,), "a", 0.58)
    add_tile((0,), "b", 0.44)
    add_tile((0,), "c", 0.44)
    add_tile((1, 3), "a", 1.0)
    add_tile((1, 3), "b", 0.72)
    add_tile((1, 3), "c", 0.72)
    add_tile((2,), "abcd", 1.3)
    add_tile((0, 1, 3), "d", 0.6)

    def positives():
        @pl.when(Y == Z // 2)
        def _():
            rc = (Z + C) % 2
            blocks = []
            for xx in range(4):
                for h in (0, 1):
                    k, j = (X - Y + 4) % 4, (xx - X + 4) % 4
                    if h == 1:
                        k, j = j, k
                    row = pl.multiple_of(jnp.where(k < 2, k, 5 - k) * 256 + h * 128 + j * HALF, HALF)
                    s = (4 * C + xx - Z + 8) % 8
                    pos = jnp.where(s == 0, 0, jnp.where(s == 4, 7, jnp.where(s < 4, 2 * s - 1, 2 * (8 - s))))
                    col = pl.multiple_of(pos * 128, 128)
                    yr = pl.multiple_of(pos * 128 + rc * ROWS + h * HALF, HALF)
                    xv = xg[pl.ds(row, HALF), :].astype(F32)
                    yv = yg[pl.ds(yr, HALF), :].astype(F32)
                    z = scale_ref[0] * jnp.sum(xv * yv, axis=1, keepdims=True) + shift_ref[0]
                    blocks.append((row, col, h, z, w[pl.ds(row, HALF), pl.ds(col, 128)]))
            less = jnp.zeros((8, 128), F32)
            lane = lax.broadcasted_iota(jnp.int32, (HALF, 128), 1)
            sub = lax.broadcasted_iota(jnp.int32, (HALF, 128), 0)
            for row, col, h, z, old in blocks:
                e = jnp.exp(z)
                wd = (e / (1.0 + e) - 1.0).astype(BF16)
                hit = lane == sub + rc * ROWS + h * HALF
                w[pl.ds(row, HALF), pl.ds(col, 128)] = jnp.where(hit, wd.astype(F32), old.astype(F32)).astype(BF16)
                less += jnp.sum(jnp.where(hit, z, 0.0).reshape(4, 8, 128), axis=0)
            lacc[...] -= less

    g.op("pos", 0.4, tiles, positives)
    fixed = ["pos"]

    def loss_axis(axis, before):
        n, me, base, kw, lat = {"c": (2, C, 0, "dc", 0.8), "z": (8, Z, 2, "dz", 4.0), "x": (4, X, 10, "dx", 2.6),
                                "y": (4, Y, 14, "dy", 2.6)}[axis]

        def run():
            if before is None:
                v = jnp.full((8, 128), jnp.sum(lacc[...]), F32)
            else:
                b, m = before
                v = lrecv[b]
                for o in range(1, m):
                    v = v + lrecv[b + o]
            lrecv[base + me] = v

        prev = {"c": "", "z": "c", "x": "z", "y": "x"}[axis]
        hops = ("zu1", "zu2", "zu3", "zu4", "zd1", "zd2", "zd3")
        deps = fixed if axis == "c" else ["l" + prev] + ([f"l{q}" for q in hops] if prev == "z" else [f"l{prev}{o}" for o in range(1, {"c": 2, "x": 4}[prev])])
        g.op("l" + axis, 0.1, deps, run)
        if axis == "z":
            for q, sign, far in (("u", 1, 4), ("d", -1, 3)):
                for t in range(1, far + 1):
                    at = base + (Z - sign * (t - 1) + 8) % 8
                    send(f"lz{q}{t}", [], 0, [f"lz{q}{t - 1}" if t > 1 else "lz"], lrecv.at[at], lrecv.at[at], dev(dz=sign), "SL")
            return
        for o in range(1, n):
            send(f"l{axis}{o}", [], 0, ["l" + axis], lrecv.at[base + me], lrecv.at[base + me], dev(**{kw: o}), "SL", "RL" + axis, lat)

    loss_axis("c", None)
    loss_axis("z", (0, 2))
    loss_axis("x", (2, 8))
    loss_axis("y", (10, 4))

    def loss_end():
        v = lrecv[14]
        for o in range(1, 4):
            v = v + lrecv[14 + o]
        lsum[...] = v
        out_ref[pl.ds(2 * ROWS, 8), pl.ds(0, 128)] = lsum[...] * (1.0 / 16384.0)

    g.op("loss", 0.1, ["ly"] + [f"ly{o}" for o in (1, 2, 3)], loss_end)

    def text(c0, nc):
        def run():
            tf[pl.ds(c0, nc), :] = lax.dot_general(w[:, pl.ds(c0, nc)], xg[...], (((0,), (0,)), ((), ())),
                                                   preferred_element_type=F32)

        return run

    for n, c0, nc, slots in (("4", 896, 128, (4,)), ("35", 640, 256, (3, 5)), ("26", 384, 256, (2, 6)),
                             ("17", 128, 256, (1, 7)), ("0", 0, 128, (0,))):
        g.op("x" + n, 0.06 + 0.52 * nc / 256, fixed, text(c0, nc))
        for s in slots:
            send(f"x{n}c{s}", ["core"], 2 * ROWS, ["x" + n], rows_of(tf, yrow(s, 1), ROWS), rows_of(crecv, s * ROWS, ROWS), dev(dc=1), "SK")

            def add(s=s):
                tf[pl.ds(yrow(s, 0), ROWS), :] += crecv[pl.ds(s * ROWS, ROWS), :]

            g.op(f"k{s}", 0.07, ["x" + n, f"x{n}c{s}"], add)

    slot = 0
    for sign, q in ((1, "p"), (-1, "m")):
        for h in pieces:
            first = 4 if (sign > 0) == (h * PIECE < HALF) else 3
            for t in range(first, 0, -1):
                s = t if sign > 0 else 8 - t
                deps = [f"k{s}"] + ([f"z{q}{t + 1}{h}"] if t < first else [])
                r = slot * PIECE

                def hop(s=s, h=h, r=r, more=t < first):
                    v = tf[pl.ds(yrow(s, 0) + h * PIECE, PIECE), :]
                    if more:
                        v = v + decode(zrecv[pl.ds(r - PIECE, PIECE), :])
                    zsend[pl.ds(r, PIECE), :] = encode(v)

                g.op(f"h{q}{t}{h}", 0.04 + 0.0014 * PIECE, deps, hop)
                send(f"z{q}{t}{h}", ["z+" if sign > 0 else "z-"], PIECE, [f"h{q}{t}{h}"], rows_of(zsend, r, PIECE), rows_of(zrecv, r, PIECE), dev(dz=sign), "SZ")
                slot += 1

            def last(h=h, r=r):
                tf[pl.ds(yrow(0, 0) + h * PIECE, PIECE), :] += decode(zrecv[pl.ds(r, PIECE), :])

            g.op(f"e{q}{h}", 0.06, ["k0", f"z{q}1{h}"], last)

    def text_end():
        out_ref[pl.ds(ROWS, ROWS), :] = restore(y_ref[...], scale_ref[0] * tf[pl.ds(yrow(0, 0), ROWS), :])

    g.op("gy", 0.3, [f"e{q}{h}" for q in "pm" for h in pieces], text_end)

    def image(k):
        def run():
            part = jnp.dot(w[pl.ds(CHUNK[k] * 256, 256), :], yg[...], preferred_element_type=F32)
            if k == 2:
                isend[pl.ds(0, 256), :] = encode(part)
                return
            imf[pl.ds(CHUNK[k] * 256, 256), :] = part
            if k:
                for b in (0, 128):
                    o = CHUNK[k] * 256 + b + (64 if k == 1 else 0)
                    isend[pl.ds(o, 64), :] = encode(imf[pl.ds(o, 64), :])

        return run

    for k in (0, 1, 2, 3):
        g.op(f"i{k}", 0.7, ["pos"], image(k))
    for q, b, ax in (("a", 0, "y"), ("b", 128, "x")):
        def part(name, start, deps, d, b=b, ax=ax, q=q):
            send(name + q, [ax + ("+" if d > 0 else "-")], HALF, deps, rows_of(isend, start + b, HALF), rows_of(irecv, start + b, HALF),
                 dev(**{"d" + ax: d}), "SI")

        ox = "x" if q == "a" else "y"
        for j in (1, 2, 0, 3):
            near, far, d = (1, 3, 1) if j in (0, 1) else (3, 1, -1)
            o2, on, of = j * HALF, CHUNK[near] * 256 + j * HALF, CHUNK[far] * 256 + j * HALF
            part(f"m2{j}", o2, ["i2"], d)
            part(f"m{far}{j}", of, [f"i{far}"], -d)

            def join(on=on, o2=o2, b=b):
                v = imf[pl.ds(on + b, HALF), :] + decode(irecv[pl.ds(o2 + b, HALF), :])
                isend[pl.ds(on + b, HALF), :] = encode(v)

            g.op(f"j{j}{q}", 0.1, [f"i{near}", f"m2{j}{q}"], join)
            part(f"m{near}{j}", on, [f"j{j}{q}"], d)
            r = (2 * (j - 1) + b // 128) * HALF

            def add_up(j=j, b=b, on=on, of=of, r=r):
                v = imf[pl.ds(b + j * HALF, HALF), :] + decode(irecv[pl.ds(on + b, HALF), :]) + decode(irecv[pl.ds(of + b, HALF), :])
                if j:
                    p2send[pl.ds(r, HALF), :] = encode(v)
                else:
                    imf[pl.ds(b, HALF), :] = v

            g.op(f"a{j}{q}", 0.12, ["i0", f"m{near}{j}{q}", f"m{far}{j}{q}"], add_up)
            if j:
                links = {1: [ox + "+"], 2: [ox + "+", ox + "-"], 3: [ox + "-"]}[j]
                send(f"n{j}{q}", links, HALF, [f"a{j}{q}"], rows_of(p2send, r, HALF), rows_of(p2recv, r, HALF), dev(**{"d" + ox: j}), "SN")

                def gather_up(j=j, b=b, r=r):
                    imf[pl.ds(b, HALF), :] += decode(p2recv[pl.ds(r, HALF), :])

                g.op(f"o{j}{q}", 0.07, ["a0" + q, f"n{j}{q}"], gather_up)

    def image_end():
        for o, b in ((0, 0), (HALF, 128)):
            out_ref[pl.ds(o, HALF), :] = restore(x_ref[pl.ds(o, HALF), :], scale_ref[0] * imf[pl.ds(b, HALF), :])

    g.op("gx", 0.4, [f"o{j}{q}" for j in (1, 2, 3) for q in "ab"], image_end)
    sizes = {"SY": zsend, "SC": rows_of(xg, 0, 512), "SX": rows_of(xg, 0, 960), "SL": rows_of(lrecv, 0, 14), "SK": crecv, "SZ": zsend,
             "SI": isend, "SN": p2send, "R4": rows_of(xg, 0, 64), "RT": rows_of(xg, 0, 256), "RLc": lrecv.at[0],
             "RLz": rows_of(lrecv, 0, 7), "RLx": rows_of(lrecv, 0, 3), "RLy": rows_of(lrecv, 0, 3)}
    for n, t in g.tasks.items():
        if t["msg"] and t["come"] not in sizes:
            sizes[t["come"]] = rows_of(xg, 0, 64)
    g.emit(ssem, rsem, sizes)


def finish(grads_ref, loss_ref, gx_ref, gy_ref):
    gx_ref[...] = grads_ref[pl.ds(0, ROWS), :]
    gy_ref[...] = grads_ref[pl.ds(ROWS, ROWS), :]
    loss_ref[0] = grads_ref[2 * ROWS, 0]


SENT = 8
COME = 123


def local(picture_embeddings, caption_embeddings, sharpness_factor, pairing_shift):
    vmem = pl.BlockSpec(memory_space=pltpu.VMEM)
    smem = pl.BlockSpec(memory_space=pltpu.SMEM)
    hbm = pl.BlockSpec(memory_space=pltpu.HBM)
    grads = pl.pallas_call(
        kernel,
        out_shape=jax.ShapeDtypeStruct((2 * ROWS + 8, D), F32),
        in_specs=[hbm, hbm, hbm, hbm],
        out_specs=vmem,
        scratch_shapes=[
            pltpu.VMEM((1024, D), BF16),
            pltpu.VMEM((1024, D), BF16),
            pltpu.VMEM((1024, 1024), BF16),
            pltpu.VMEM((768, D), F32),
            pltpu.VMEM((768, D), BF16),
            pltpu.VMEM((768, D), BF16),
            pltpu.VMEM((192, D), BF16),
            pltpu.VMEM((192, D), BF16),
            pltpu.VMEM((1024, D), F32),
            pltpu.VMEM((512, D), F32),
            pltpu.VMEM((448, D), BF16),
            pltpu.VMEM((448, D), BF16),
            pltpu.VMEM((8, 128), F32),
            pltpu.VMEM((8, 128), F32),
            pltpu.VMEM((18, 8, 128), F32),
            pltpu.VMEM((ROWS, D), BF16),
            pltpu.VMEM((ROWS, D), BF16),
            pltpu.SMEM((1,), F32),
            pltpu.SMEM((1,), F32),
            pltpu.SemaphoreType.DMA((4,)),
            pltpu.SemaphoreType.DMA((SENT,)),
            pltpu.SemaphoreType.DMA((COME,)),
        ],
        compiler_params=pltpu.CompilerParams(collective_id=0, has_side_effects=True, vmem_limit_bytes=40 * 2**20),
    )(picture_embeddings, caption_embeddings, sharpness_factor, pairing_shift)
    return pl.pallas_call(
        finish,
        out_shape=(
            jax.ShapeDtypeStruct((1,), F32),
            jax.ShapeDtypeStruct((ROWS, D), F32),
            jax.ShapeDtypeStruct((ROWS, D), F32),
        ),
        in_specs=[vmem],
        out_specs=(smem, vmem, vmem),
        compiler_params=pltpu.CompilerParams(vmem_limit_bytes=4 * 2**20),
    )(grads)


def solution(mesh):
    in_specs = (P(("img", "txt"), None), P(("txt", "img"), None), P(), P())
    out_specs = (P(), P(("img", "txt"), None), P(("txt", "img"), None))
    return jax.shard_map(local, mesh=mesh, in_specs=in_specs, out_specs=out_specs, check_vma=False)
```
